256 devices in a mesh: row: 16 (over x, y), col: 16 (over z, core).
Axes of the slice: x: 4, y: 4, z: 8, core: 2. Of those that a mesh axis runs over, the one named last changes fastest.
Arguments:
- tokens: bfloat16 [2048, 8192], P('col', 'row'), may hold values from -6 to 6
- grad_out: bfloat16 [2048, 8192], P('col', 'row'), may hold values from -0.59765625 to 0.59765625
- gate_weight: bfloat16 [8192, 14336], P('row', 'col'), may hold values from -0.09375 to 0.09375
- up_weight: bfloat16 [8192, 14336], P('row', 'col'), may hold values from -0.09375 to 0.09375
- down_weight: bfloat16 [14336, 8192], P('col', 'row'), may hold values from -0.0625 to 0.0625
- gate_mask: int32 [64, 112], P('row', 'col'), may hold values from 0 to 1, as said below
- up_mask: int32 [64, 112], P('row', 'col'), may hold values from 0 to 1, as said below
- down_mask: int32 [112, 64], P('col', 'row'), may hold values from 0 to 1, as said below
Outputs:
- layer_output: bfloat16 [2048, 8192], P('col', 'row')
- input_grad: bfloat16 [2048, 8192], P('col', 'row')
- gate_grad: bfloat16 [8192, 14336], P('row', 'col')
- up_grad: bfloat16 [8192, 14336], P('row', 'col')
- down_grad: bfloat16 [14336, 8192], P('col', 'row')
The draws below stay inside these ranges and needn't reach their ends.
Inputs may be any that keep to these rules, and one draw needn't show every extreme that they name: `gate_mask`: 1 marks a live block of 128 x 128 weights, 0 a pruned one. `up_mask`: 1 marks a live block of 128 x 128 weights, 0 a pruned one. `down_mask`: 1 marks a live block of 128 x 128 weights, 0 a pruned one.
All inputs are finite; a program needn't handle non-finite values.
Results may differ from the reference program's by a relative error of at most 0.035.
Values may be sent and summed in bfloat16 or wider, within the bound.
A program may use at most 128 MiB of HBM per device.

```python
import jax
import jax.numpy as jnp
from jax import lax

D = 8192
FF = 14336
BLK = 128
TOKENS = 2048
N_ROW = 16


def mask_levels(key, block_rows, block_cols):
    first_key, second_key, third_key = jax.random.split(key, 3)
    row_level = jax.random.randint(first_key, (block_rows, 1), 50, 450)
    col_level = jax.random.randint(second_key, (1, block_cols), 50, 450)
    ticket = jax.random.randint(third_key, (block_rows, block_cols), 0, 1000)
    return (ticket < row_level + col_level).astype(jnp.int32)


def draw_gate_mask(key, part):
    key = jax.random.fold_in(key, 11)
    return mask_levels(key, D // BLK, FF // BLK)


def draw_up_mask(key, part):
    key = jax.random.fold_in(key, 23)
    return mask_levels(key, D // BLK, FF // BLK)


def draw_down_mask(key, part):
    key = jax.random.fold_in(key, 37)
    return mask_levels(key, FF // BLK, D // BLK)


def with_spikes(values, own_key, source, target, shards_of, factor):
    owner, partner = [(jnp.arange(values.shape[axis_at]) // (values.shape[axis_at] // shards_of)).reshape([-1 if axis == axis_at else 1 for axis in range(values.ndim)]) for axis_at in (source, target)]
    chosen = jax.random.permutation(own_key, shards_of)[partner]
    strong = (owner == chosen) | (owner == (partner + shards_of // 2) % shards_of)
    return jnp.where(strong, factor * values, values)


def shard_levels(stream_key, extent, cuts, low, top_value):
    gain, own = 1.0, jax.random.fold_in(stream_key, 6)
    for axis_at, blocks in cuts:
        steps = jnp.exp(jax.random.uniform(jax.random.fold_in(own, axis_at), (blocks,), jnp.float32, low / len(cuts), top_value / len(cuts)))
        gain = gain * jnp.repeat(steps, extent[axis_at] // blocks).reshape([-1 if axis == axis_at else 1 for axis in range(len(extent))])
    return gain


def normal_values(key, extent, deviation, bound, cuts=(), held_as=jnp.bfloat16):
    entries = deviation * jax.random.normal(key, extent, jnp.float32)
    if cuts:
        entries = entries * shard_levels(key, extent, cuts, -0.22, 0.18)
    return jnp.clip(entries, -bound, bound).astype(held_as)


def noise_with(stream_key, shape, width, bound, cuts, heavy, held_as=jnp.bfloat16):
    entries = width * jax.random.normal(stream_key, shape, jnp.float32)
    if cuts:
        entries = entries * shard_levels(stream_key, shape, cuts, -0.22, 0.18)
    return jnp.clip(with_spikes(entries, jax.random.fold_in(stream_key, 3), *heavy), -bound, bound).astype(held_as)


def setup_inputs(seed: int = 0) -> dict:
    key_of = jax.random.split(jax.random.key(seed), 9)
    tokens = noise_with(key_of[0], (TOKENS, D), 1.0, 6.0, ((0, 16), (1, 16)), (1, 0, 16, 2.0))
    grad_out = noise_with(key_of[1], (TOKENS, D), 0.1, 0.59765625, ((0, 16), (1, 16)), (1, 0, 16, 2.0))
    gate_weight = normal_values(key_of[2], (D, FF), (D // 2) ** -0.5, 0.09375, ((0, 16), (1, 16)))
    up_weight = normal_values(key_of[3], (D, FF), (D // 2) ** -0.5, 0.09375, ((0, 16), (1, 16)))
    down_weight = normal_values(key_of[4], (FF, D), (FF // 2) ** -0.5, 0.0625, ((0, 16), (1, 16)))
    gate_mask = draw_gate_mask(jax.random.fold_in(key_of[8], 71), 0)
    up_mask = draw_up_mask(jax.random.fold_in(key_of[8], 71), 0)
    down_mask = draw_down_mask(jax.random.fold_in(key_of[8], 71), 0)
    return dict(tokens=tokens, grad_out=grad_out, gate_weight=gate_weight, up_weight=up_weight, down_weight=down_weight, gate_mask=gate_mask, up_mask=up_mask, down_mask=down_mask)


def expand_mask(mask_tile, weight_tile):
    blocks_a, blocks_b = mask_tile.shape
    scaled = mask_tile.astype(weight_tile.dtype)[:, None, :, None]
    return (weight_tile.reshape(blocks_a, BLK, blocks_b, BLK) * scaled).reshape(weight_tile.shape)


def block_sums(left_mat, right_mat, pieces):
    inner = left_mat.shape[1] // pieces

    def add_piece(block_idx, running):
        offset = (block_idx * inner).astype(jnp.int32)
        left_part = lax.dynamic_slice_in_dim(left_mat, offset, inner, 1)
        right_part = lax.dynamic_slice_in_dim(right_mat, offset, inner, 0)
        partial_sum = jnp.dot(left_part, right_part, preferred_element_type=jnp.float32)
        rounded = lax.optimization_barrier(partial_sum.astype(jnp.bfloat16))
        return running + rounded.astype(jnp.float32)

    start_value = jnp.zeros((left_mat.shape[0], right_mat.shape[1]), jnp.float32)
    return lax.fori_loop(0, pieces, add_piece, start_value)


def reference(tokens, grad_out, gate_weight, up_weight, down_weight, gate_mask, up_mask, down_mask):
    pruned_gate = expand_mask(gate_mask, gate_weight)
    pruned_up = expand_mask(up_mask, up_weight)
    pruned_down = expand_mask(down_mask, down_weight)
    gate_up_w = jnp.concatenate((pruned_gate, pruned_up), 1)
    gate_up = block_sums(tokens, gate_up_w, N_ROW).astype(jnp.bfloat16)
    gate_act = gate_up[:, :FF].astype(jnp.float32)
    up_act = gate_up[:, FF:].astype(jnp.float32)
    sigmoid_g = jax.nn.sigmoid(gate_act)
    silu_g = gate_act * sigmoid_g
    slope_g = sigmoid_g * (1.0 + gate_act * (1.0 - sigmoid_g))
    hidden = (silu_g * up_act).astype(jnp.bfloat16)
    layer_output = jnp.dot(hidden, pruned_down, preferred_element_type=jnp.float32).astype(jnp.bfloat16)
    hidden_grad = block_sums(grad_out, pruned_down.T, N_ROW)
    gate_act_grad = (hidden_grad * up_act * slope_g).astype(jnp.bfloat16)
    up_act_grad = (hidden_grad * silu_g).astype(jnp.bfloat16)
    down_grad = expand_mask(down_mask, jnp.dot(hidden.T, grad_out, preferred_element_type=jnp.float32)).astype(jnp.bfloat16)
    gate_grad = expand_mask(gate_mask, jnp.dot(tokens.T, gate_act_grad, preferred_element_type=jnp.float32)).astype(jnp.bfloat16)
    up_grad = expand_mask(up_mask, jnp.dot(tokens.T, up_act_grad, preferred_element_type=jnp.float32)).astype(jnp.bfloat16)
    both_grads = jnp.concatenate((gate_act_grad, up_act_grad), 1)
    input_grad = jnp.dot(both_grads, gate_up_w.T, preferred_element_type=jnp.float32).astype(jnp.bfloat16)
    return (layer_output, input_grad, gate_grad, up_grad, down_grad)
```

```python
import jax
import jax.numpy as jnp
from jax import lax
from jax.experimental import pallas as pl
from jax.experimental.pallas import tpu as pltpu
from jax.sharding import PartitionSpec as P

BLK = 128
NX, NY, NZ = 4, 4, 8
F = 896
D = 512
F32, BF = jnp.float32, jnp.bfloat16
MESH = pl.DeviceIdType.MESH
NSEM = 200


def rows_of(ref, *lead):
    value = ref[lead]
    return value.reshape(256, value.shape[-1])


def dot_nn(a, b):
    return jnp.dot(a, b, preferred_element_type=F32)


def dot_nt(a, b):
    return lax.dot_general(a, b, (((1,), (1,)), ((), ())), preferred_element_type=F32)


class Link:
    def __init__(self, send_sem, recv_sem):
        self.send_sem, self.recv_sem, self.copies = send_sem, recv_sem, []

    def send(self, src, dst, device):
        at = len(self.copies)
        copy = pltpu.make_async_remote_copy(
            src_ref=src, dst_ref=dst, send_sem=self.send_sem.at[at], recv_sem=self.recv_sem.at[at],
            device_id=device, device_id_type=MESH,
        )
        copy.start()
        self.copies.append(copy)
        return copy

    def drain(self):
        for copy in self.copies:
            copy.wait_send()


class GatherZ:
    def __init__(self, link, where, full, own):
        self.link, self.w, self.full, self.own = link, where, full, own

    def slot(self, k, *half):
        chunk = lax.rem(self.w.z + k + NZ, NZ) * 2 + self.w.core
        return self.full.at[(lax.div(chunk, 4), lax.rem(chunk, 4), *half)]

    def start(self):
        own = self.slot(0)
        own[...] = self.own[...]
        self.right = [self.link.send(own, own, self.w.Z(1))]
        self.left = [self.link.send(own, own, self.w.Z(-1))]
        self.side = [self.link.send(own, own, self.w.sibling)]

    def step(self, k):
        for copies, sign, half in ((self.right, -1, 0), (self.left, 1, 1)):
            copies[k - 1].wait_recv()
            got = self.slot(sign * k)
            on = got if k < 3 else self.slot(sign * k, half)
            copies.append(self.link.send(on, on, self.w.Z(-sign)))
            self.side.append(self.link.send(got, got, self.w.sibling))

    def last(self):
        self.right[3].wait_recv()
        self.left[3].wait_recv()
        got = self.slot(4)
        self.side.append(self.link.send(got, got, self.w.sibling))

    def finish(self):
        for copy in self.side:
            copy.wait_recv()


class ScatterXY:
    def __init__(self, link, where, half, full, bufs):
        self.link, self.half, self.full = link, half, full
        self.r1, self.r2, self.s, self.q1, self.q2 = bufs
        if half == 0:
            self.m, self.o, self.first, self.second = where.x, where.y, where.X, where.Y
        else:
            self.m, self.o, self.first, self.second = where.y, where.x, where.Y, where.X

    def index(self, k, *other):
        d = lax.rem(self.m + k + 4, 4)
        o = other[0] if other else slice(None)
        return (d, o, self.half) if self.half == 0 else (o, d, self.half)

    def opposite(self):
        lo, hi = (self.full.at[self.index(2, slice(a, a + 2))] for a in (0, 2))
        self.a_p = self.link.send(lo, self.r1.at[0], self.first(1))
        self.a_m = self.link.send(hi, self.r1.at[1], self.first(-1))

    def raw(self):
        hi = self.full.at[self.index(1, slice(2, 4))]
        lo = self.full.at[self.index(-1, slice(0, 2))]
        self.b_p = self.link.send(hi, self.r2.at[0, 2:4], self.first(1))
        self.b_m = self.link.send(lo, self.r2.at[1, 0:2], self.first(-1))

    def sums(self):
        self.a_p.wait_recv()
        for i in range(2):
            at = self.index(1, i)
            self.full[at] = (self.full[at].astype(F32) + self.r1[0, i].astype(F32)).astype(BF)
        src = self.full.at[self.index(1, slice(0, 2))]
        self.c_p = self.link.send(src, self.r2.at[0, 0:2], self.first(1))
        self.a_m.wait_recv()
        for i in range(2):
            at = self.index(-1, i + 2)
            self.full[at] = (self.full[at].astype(F32) + self.r1[1, i].astype(F32)).astype(BF)
        src = self.full.at[self.index(-1, slice(2, 4))]
        self.c_m = self.link.send(src, self.r2.at[1, 2:4], self.first(-1))

    def middle(self):
        for copy in (self.b_p, self.b_m, self.c_p, self.c_m):
            copy.wait_recv()
        for k in (2, 1, 3, 0):
            i = lax.rem(self.o + k, 4)
            at = self.index(0, i)
            self.s[i] = (
                self.full[at].astype(F32) + self.r2[0, i].astype(F32) + self.r2[1, i].astype(F32)
            ).astype(BF)
        p, q, m = (lax.rem(self.o + k, 4) for k in (1, 2, 3))
        self.d_p = self.link.send(self.s.at[q, 0:32], self.q1.at[0], self.second(1))
        self.d_m = self.link.send(self.s.at[q, 32:64], self.q1.at[1], self.second(-1))
        self.e_p = self.link.send(self.s.at[p, 32:64], self.q2.at[0, 32:64], self.second(1))
        self.e_m = self.link.send(self.s.at[m, 0:32], self.q2.at[1, 0:32], self.second(-1))

    def sums2(self):
        p, m = (lax.rem(self.o + k, 4) for k in (1, 3))
        self.d_p.wait_recv()
        self.s[p, 0:32] = (self.s[p, 0:32].astype(F32) + self.q1[0].astype(F32)).astype(BF)
        self.f_p = self.link.send(self.s.at[p, 0:32], self.q2.at[0, 0:32], self.second(1))
        self.d_m.wait_recv()
        self.s[m, 32:64] = (self.s[m, 32:64].astype(F32) + self.q1[1].astype(F32)).astype(BF)
        self.f_m = self.link.send(self.s.at[m, 32:64], self.q2.at[1, 32:64], self.second(-1))

    def arrive(self):
        for copy in (self.e_p, self.e_m, self.f_p, self.f_m):
            copy.wait_recv()

    def result(self, cols):
        return (
            self.s[self.o, :, cols].astype(F32)
            + self.q2[0, :, cols].astype(F32)
            + self.q2[1, :, cols].astype(F32)
        )


class GatherXY:
    def __init__(self, link, where, half, full):
        self.link, self.half, self.full = link, half, full
        if half == 0:
            self.m, self.o, self.first, self.second = where.x, where.y, where.X, where.Y
        else:
            self.m, self.o, self.first, self.second = where.y, where.x, where.Y, where.X
        self.p, self.q = [], []

    def at(self, k, j, *rows):
        a, b = lax.rem(self.m + k + 4, 4), lax.rem(self.o + j + 4, 4)
        return self.full.at[(a, b, self.half, *rows) if self.half == 0 else (b, a, self.half, *rows)]

    def send(self, ref, device):
        return self.link.send(ref, ref, device)

    def across(self, k):
        piece = self.at(k, 0)
        self.p.append(self.send(piece, self.second(1)))
        self.q.append(self.send(piece, self.second(-1)))

    def start(self):
        piece = self.at(0, 0)
        self.a_p = self.send(piece, self.first(1))
        self.a_m = self.send(piece, self.first(-1))
        self.across(0)

    def near(self):
        self.a_p.wait_recv()
        self.b_p = self.send(self.at(-1, 0, slice(0, 32)), self.first(1))
        self.a_m.wait_recv()
        self.b_m = self.send(self.at(1, 0, slice(32, 64)), self.first(-1))
        self.across(-1)
        self.across(1)

    def far(self):
        self.b_p.wait_recv()
        self.b_m.wait_recv()
        self.across(2)

    def relay(self, n):
        k = (0, -1, 1, 2)[n]
        self.p[n].wait_recv()
        self.p[n] = self.send(self.at(k, -1, slice(0, 32)), self.second(1))
        self.q[n].wait_recv()
        self.q[n] = self.send(self.at(k, 1, slice(32, 64)), self.second(-1))

    def finish(self):
        for copy in self.p + self.q:
            copy.wait_recv()

    def group(self, j):
        b = lax.rem(self.o + j + 4, 4)
        return (slice(None), b, self.half) if self.half == 0 else (b, slice(None), self.half)


class ScatterZ:
    def __init__(self, link, where, full, side, right, left, out):
        self.link, self.w, self.full, self.side = link, where, full, side
        self.right, self.left, self.out = right, left, out

    def swap(self):
        other = 1 - self.w.core
        self.pair = [
            self.link.send(self.full.at[:, other + 2 * j], self.side.at[:, j], self.w.sibling)
            for j in range(2)
        ]

    def both(self, k, half):
        to = lax.rem(self.w.z + k + NZ, NZ)
        a, j = lax.div(to, 2), lax.rem(to, 2)
        at = (a, 2 * j + self.w.core, half)
        return at, self.full[at].astype(F32) + self.side[a, j, half].astype(F32)

    def chunk(self, k):
        to = lax.rem(self.w.z + k + NZ, NZ)
        return self.full.at[lax.div(to, 2), 2 * lax.rem(to, 2) + self.w.core]

    def begin(self):
        for copy in self.pair:
            copy.wait_recv()
        self.moves = []
        for half, buf, way in ((0, self.right, 1), (1, self.left, -1)):
            at, total = self.both(4, half)
            self.full[at] = total.astype(BF)
            self.moves.append(self.link.send(self.full.at[at], buf.at[0, half], self.w.Z(way)))

    def step(self, n):
        for i, (buf, way) in enumerate(((self.right, 1), (self.left, -1))):
            self.moves[i].wait_recv()
            for half in range(2):
                at, total = self.both(way * (4 - n), half)
                if n > 1 or half == i:
                    total = total + buf[n - 1, half].astype(F32)
                self.full[at] = total.astype(BF)
            self.moves[i] = self.link.send(self.chunk(way * (4 - n)), buf.at[n], self.w.Z(way))

    def finish(self):
        for copy in self.moves:
            copy.wait_recv()
        for half in range(2):
            total = self.both(0, half)[1]
            self.out[half] = (
                total + self.right[3, half].astype(F32) + self.left[3, half].astype(F32)
            ).astype(BF)


class Where:
    def __init__(self):
        r, c = lax.axis_index("row"), lax.axis_index("col")
        self.r, self.c = r, c
        self.x, self.y = lax.div(r, NY), lax.rem(r, NY)
        self.z, self.core = lax.div(c, 2), lax.rem(c, 2)
        self.sibling = (r, 2 * self.z + 1 - self.core)

    def X(self, k):
        return (lax.rem(self.x + k + NX, NX) * NY + self.y, self.c)

    def Y(self, k):
        return (self.x * NY + lax.rem(self.y + k + NY, NY), self.c)

    def Z(self, k):
        return (self.r, lax.rem(self.z + k + NZ, NZ) * 2 + self.core)


def kernel(
    tok, go, wg, wu, wd, gm, um, dm,
    lo, ig, gg, dgt,
    t_all, g_all, tt, gt, w, wdm, p_gu, p_hg,
    ra1, ra2, sa, qa1, qa2, rb1, rb2, sb, qb1, qb2,
    ha1, ha2, hsa, hqa1, hqa2, hb1, hb2, hsb, hqb1, hqb2,
    hid, gr, silu_s, slope_s, lop, igp, lo_side, ig_side, lo_r, lo_l, ig_r, ig_l,
    send_sem, recv_sem, load_sem,
):
    where = Where()
    link = Link(send_sem, recv_sem)

    loads = [
        pltpu.make_async_copy(wg, w.at[:, 0:F], load_sem.at[0]),
        pltpu.make_async_copy(wu, w.at[:, F : 2 * F], load_sem.at[1]),
        pltpu.make_async_copy(wd, wdm, load_sem.at[2]),
    ]
    for load in loads:
        load.start()

    barrier = pltpu.get_barrier_semaphore()
    near = (where.X(1), where.X(-1), where.Y(1), where.Y(-1), where.Z(1), where.Z(-1), where.sibling)
    for device in near:
        pl.semaphore_signal(barrier, inc=1, device_id=device, device_id_type=MESH)
    pl.semaphore_wait(barrier, len(near))

    tz = GatherZ(link, where, t_all, tok)
    gz = GatherZ(link, where, g_all, go)
    tz.start()

    for load in loads:
        load.wait()

    @pl.loop(0, 4)
    def _(i):
        rows = pl.ds(pl.multiple_of(i * BLK, BLK), BLK)
        for m_ref, base in ((gm, 0), (um, F)):
            for j in range(7):
                cols = pl.ds(base + j * BLK, BLK)
                w[rows, cols] = (w[rows, cols].astype(F32) * m_ref[i, j].astype(F32)).astype(BF)

    tz.step(1)

    @pl.loop(0, 7)
    def _(i):
        rows = pl.ds(pl.multiple_of(i * BLK, BLK), BLK)
        for j in range(4):
            cols = pl.ds(j * BLK, BLK)
            wdm[rows, cols] = (wdm[rows, cols].astype(F32) * dm[i, j].astype(F32)).astype(BF)

    tz.step(2)
    tz.step(3)
    gz.start()
    tz.last()
    tz.finish()

    gu = [
        ScatterXY(link, where, 0, p_gu, (ra1, ra2, sa, qa1, qa2)),
        ScatterXY(link, where, 1, p_gu, (rb1, rb2, sb, qb1, qb2)),
    ]
    hg = [
        ScatterXY(link, where, 0, p_hg, (ha1, ha2, hsa, hqa1, hqa2)),
        ScatterXY(link, where, 1, p_hg, (hb1, hb2, hsb, hqb1, hqb2)),
    ]

    def part_gu(s, k):
        at = s.index(k)

        @pl.loop(0, 2)
        def _(n):
            cols = pl.ds(pl.multiple_of(n * F, BLK), F)
            part = dot_nn(rows_of(t_all, *at), w[:, cols])
            p_gu[(*at, slice(None), cols)] = part.astype(BF).reshape(4, 64, F)

    def part_hg(s, k):
        at = s.index(k)
        p_hg[at] = dot_nt(rows_of(g_all, *at), wdm[...]).astype(BF).reshape(4, 64, F)

    for s in gu:
        part_gu(s, 2)
        s.opposite()
    gz.step(1)
    for s in gu:
        part_gu(s, 1)
        part_gu(s, -1)
        s.raw()
    gz.step(2)
    for s in gu:
        part_gu(s, 0)
    gz.step(3)

    def transpose(src, dst):
        @pl.loop(0, 16)
        def _(c):
            block = src[lax.div(c, 4), lax.rem(c, 4)].reshape(BLK, D)
            dst[:, pl.ds(pl.multiple_of(c * BLK, BLK), BLK)] = block.T

    transpose(t_all, tt)
    gz.last()
    gz.finish()
    for s in hg:
        part_hg(s, 2)
        s.opposite()
    for s in gu:
        s.sums()
    for s in hg:
        part_hg(s, 1)
        part_hg(s, -1)
        s.raw()
    for s in hg:
        part_hg(s, 0)
    transpose(g_all, gt)
    for s in gu:
        s.middle()
    for s in hg:
        s.sums()
    for s in gu:
        s.sums2()
    for s in hg:
        s.middle()

    hid_ag = [GatherXY(link, where, h, hid) for h in range(2)]
    gr_ag = [GatherXY(link, where, h, gr) for h in range(2)]
    for h in range(2):
        gu[h].arrive()
        gate = gu[h].result(slice(0, F)).astype(BF).astype(F32)
        up = gu[h].result(slice(F, 2 * F)).astype(BF).astype(F32)
        sig = 1.0 / (1.0 + jnp.exp(-gate))
        silu = gate * sig
        silu_s[h] = silu
        slope_s[h] = up * (sig * (1.0 + gate * (1.0 - sig)))
        hid[where.x, where.y, h] = (silu * up).astype(BF)
        hid_ag[h].start()
    for s in hg:
        s.sums2()
    for a in hid_ag:
        a.near()
    for h in range(2):
        hg[h].arrive()
        hgrad = hg[h].result(slice(0, F))
        gr[where.x, where.y, h, :, 0:F] = (hgrad * slope_s[h]).astype(BF)
        gr[where.x, where.y, h, :, F : 2 * F] = (hgrad * silu_s[h]).astype(BF)
        gr_ag[h].start()
    for a in hid_ag:
        a.far()
    for n in range(2):
        for a in hid_ag:
            a.relay(n)
    for a in gr_ag:
        a.near()
    for n in range(2, 4):
        for a in hid_ag:
            a.relay(n)
    for a in gr_ag:
        a.far()
    for a in hid_ag:
        a.finish()

    lz = ScatterZ(link, where, lop, lo_side, lo_r, lo_l, lo)
    iz = ScatterZ(link, where, igp, ig_side, ig_r, ig_l, ig)

    def out_part(a):
        @pl.loop(0, 4)
        def _(j):
            b = j
            at = (slice(None), b, a.half) if a.half == 0 else (b, slice(None), a.half)
            lop[at] = dot_nn(rows_of(hid, *at), wdm[...]).astype(BF).reshape(4, 64, D)

    def in_part(a, j):
        at = a.group(j)
        igp[at] = dot_nt(rows_of(gr, *at), w[...]).astype(BF).reshape(4, 64, D)

    out_part(hid_ag[0])
    for a in gr_ag:
        a.relay(0)
    out_part(hid_ag[1])
    lz.swap()
    for a in gr_ag:
        in_part(a, 0)
    lz.begin()
    for a in gr_ag:
        a.relay(1)
    lz.step(1)

    @pl.loop(0, 7)
    def _(n):
        cols = pl.ds(pl.multiple_of(n * BLK, BLK), BLK)
        right = hid[:, :, :, :, cols].reshape(2048, BLK)
        dgt[:, cols] = dot_nn(gt[...], right).astype(BF)

    lz.step(2)
    for a in gr_ag:
        a.relay(2)
    lz.step(3)
    for a in gr_ag:
        a.relay(3)
    lz.finish()
    for a in gr_ag:
        in_part(a, -1)
        in_part(a, 1)
    for a in gr_ag:
        a.finish()
        in_part(a, 2)
    iz.swap()

    def weight_part(first, last):
        @pl.loop(first, last)
        def _(n):
            cols = pl.ds(pl.multiple_of(n * 256, 256), 256)
            right = gr[:, :, :, :, cols].reshape(2048, 256)
            gg[:, cols] = dot_nn(tt[...], right).astype(BF)

    weight_part(0, 2)
    iz.begin()
    weight_part(2, 4)
    iz.step(1)
    weight_part(4, 6)
    iz.step(2)
    weight_part(6, 7)
    iz.step(3)
    iz.finish()
    link.drain()


def scatter_bufs(n):
    return [
        pltpu.VMEM((2, 2, 64, n), BF),
        pltpu.VMEM((2, 4, 64, n), BF),
        pltpu.VMEM((4, 64, n), BF),
        pltpu.VMEM((2, 32, n), BF),
        pltpu.VMEM((2, 64, n), BF),
    ]


def expand_mask(mask_tile, tile):
    blocks_a, blocks_b = mask_tile.shape
    scaled = mask_tile.astype(tile.dtype)[:, None, :, None]
    return (tile.reshape(blocks_a, BLK, blocks_b, BLK) * scaled).reshape(tile.shape)


def body(tokens, grad_out, gate_weight, up_weight, down_weight, gate_mask, up_mask, down_mask):
    vmem = pl.BlockSpec(memory_space=pltpu.VMEM)
    smem = pl.BlockSpec(memory_space=pltpu.SMEM)
    anywhere = pl.BlockSpec(memory_space=pl.ANY)
    chunks = (4, 4, 2, 64)
    lo, ig, gg, dgt = pl.pallas_call(
        kernel,
        out_shape=(
            jax.ShapeDtypeStruct((2, 64, D), BF),
            jax.ShapeDtypeStruct((2, 64, D), BF),
            jax.ShapeDtypeStruct((D, 2 * F), BF),
            jax.ShapeDtypeStruct((D, F), BF),
        ),
        in_specs=[vmem, vmem, anywhere, anywhere, anywhere, smem, smem, smem],
        out_specs=(vmem, vmem, vmem, vmem),
        scratch_shapes=[
            pltpu.VMEM((*chunks, D), BF),
            pltpu.VMEM((*chunks, D), BF),
            pltpu.VMEM((D, 2048), BF),
            pltpu.VMEM((D, 2048), BF),
            pltpu.VMEM((D, 2 * F), BF),
            pltpu.VMEM((F, D), BF),
            pltpu.VMEM((*chunks, 2 * F), BF),
            pltpu.VMEM((*chunks, F), BF),
            *scatter_bufs(2 * F), *scatter_bufs(2 * F),
            *scatter_bufs(F), *scatter_bufs(F),
            pltpu.VMEM((*chunks, F), BF),
            pltpu.VMEM((*chunks, 2 * F), BF),
            pltpu.VMEM((2, 64, F), F32),
            pltpu.VMEM((2, 64, F), F32),
            pltpu.VMEM((*chunks, D), BF),
            pltpu.VMEM((*chunks, D), BF),
            pltpu.VMEM((4, 2, 2, 64, D), BF),
            pltpu.VMEM((4, 2, 2, 64, D), BF),
            *[pltpu.VMEM((4, 2, 64, D), BF)] * 4,
            pltpu.SemaphoreType.DMA((NSEM,)),
            pltpu.SemaphoreType.DMA((NSEM,)),
            pltpu.SemaphoreType.DMA((3,)),
        ],
        compiler_params=pltpu.CompilerParams(
            collective_id=0, has_side_effects=True, vmem_limit_bytes=63 * 2**20
        ),
        cost_estimate=pl.CostEstimate(flops=2 * 9 * 2048 * D * F, bytes_accessed=8 * 2**20, transcendentals=0),
    )(
        tokens.reshape(2, 64, D), grad_out.reshape(2, 64, D), gate_weight, up_weight, down_weight,
        gate_mask, up_mask, down_mask,
    )
    return (
        lo.reshape(BLK, D),
        ig.reshape(BLK, D),
        expand_mask(gate_mask, gg[:, :F]),
        expand_mask(up_mask, gg[:, F:]),
        expand_mask(down_mask, dgt.T),
    )


def solution(mesh):
    wide, tall = P("row", "col"), P("col", "row")
    return jax.shard_map(
        body,
        mesh=mesh,
        in_specs=(tall, tall, wide, wide, tall, wide, wide, tall),
        out_specs=(tall, tall, wide, wide, tall),
        check_vma=False,
    )
```

```python
import jax
import jax.numpy as jnp
from jax import lax
from jax.experimental import pallas as pl
from jax.experimental.pallas import tpu as pltpu
from jax.sharding import PartitionSpec as P

BLK = 128
NX, NY, NZ = 4, 4, 8
F = 896
D = 512
F32, BF = jnp.float32, jnp.bfloat16
MESH = pl.DeviceIdType.MESH
NSEM = 240


def rows_of(ref, *lead):
    value = ref[lead]
    return value.reshape(256, value.shape[-1])


def dot_nn(a, b):
    return jnp.dot(a, b, preferred_element_type=F32)


def dot_nt(a, b):
    return lax.dot_general(a, b, (((1,), (1,)), ((), ())), preferred_element_type=F32)


class Link:
    def __init__(self, send_sem, recv_sem):
        self.send_sem, self.recv_sem, self.copies = send_sem, recv_sem, []

    def send(self, src, dst, device):
        at = len(self.copies)
        copy = pltpu.make_async_remote_copy(
            src_ref=src, dst_ref=dst, send_sem=self.send_sem.at[at], recv_sem=self.recv_sem.at[at],
            device_id=device, device_id_type=MESH,
        )
        copy.start()
        self.copies.append(copy)
        return copy

    def drain(self):
        for copy in self.copies:
            copy.wait_send()


class GatherZ:
    def __init__(self, link, where, full, own):
        self.link, self.w, self.full, self.own = link, where, full, own
        self.moves = {}

    def slot(self, k, *half):
        chunk = lax.rem(self.w.z + k + NZ, NZ) * 2 + self.w.core
        return self.full.at[(lax.div(chunk, 4), lax.rem(chunk, 4), *half)]

    def move(self, way, k, half):
        ref = self.slot(k, half)
        self.moves[way, half] = self.link.send(ref, ref, self.w.Z(way))

    def start(self):
        own = self.slot(0)
        own[...] = self.own[...]
        for half in range(2):
            for way in (1, -1):
                self.move(way, 0, half if way == 1 else 1 - half)
        self.side = [self.link.send(own, own, self.w.sibling)]

    def step(self, k):
        for turn in range(2):
            for way in (1, -1):
                half = turn if way == 1 else 1 - turn
                self.moves[way, half].wait_recv()
                if k < 3 or turn == 0:
                    self.move(way, -way * k, half)
        for way in (1, -1):
            got = self.slot(-way * k)
            self.side.append(self.link.send(got, got, self.w.sibling))

    def last(self):
        self.moves[1, 0].wait_recv()
        self.moves[-1, 1].wait_recv()
        got = self.slot(4)
        self.side.append(self.link.send(got, got, self.w.sibling))

    def finish(self):
        for copy in self.side:
            copy.wait_recv()


class ScatterXY:
    def __init__(self, link, where, half, full, bufs):
        self.link, self.half, self.full = link, half, full
        self.r1, self.r2, self.s, self.q1, self.q2 = bufs
        if half == 0:
            self.m, self.o, self.first, self.second = where.x, where.y, where.X, where.Y
        else:
            self.m, self.o, self.first, self.second = where.y, where.x, where.Y, where.X

    def index(self, k, *other):
        d = lax.rem(self.m + k + 4, 4)
        o = other[0] if other else slice(None)
        return (d, o, self.half) if self.half == 0 else (o, d, self.half)

    def opposite(self):
        lo, hi = (self.full.at[self.index(2, slice(a, a + 2))] for a in (0, 2))
        self.a_p = self.link.send(lo, self.r1.at[0], self.first(1))
        self.a_m = self.link.send(hi, self.r1.at[1], self.first(-1))

    def raw(self):
        hi = self.full.at[self.index(1, slice(2, 4))]
        lo = self.full.at[self.index(-1, slice(0, 2))]
        self.b_p = self.link.send(hi, self.r2.at[0, 2:4], self.first(1))
        self.b_m = self.link.send(lo, self.r2.at[1, 0:2], self.first(-1))

    def sums(self):
        self.a_p.wait_recv()
        for i in range(2):
            at = self.index(1, i)
            self.full[at] = (self.full[at].astype(F32) + self.r1[0, i].astype(F32)).astype(BF)
        src = self.full.at[self.index(1, slice(0, 2))]
        self.c_p = self.link.send(src, self.r2.at[0, 0:2], self.first(1))
        self.a_m.wait_recv()
        for i in range(2):
            at = self.index(-1, i + 2)
            self.full[at] = (self.full[at].astype(F32) + self.r1[1, i].astype(F32)).astype(BF)
        src = self.full.at[self.index(-1, slice(2, 4))]
        self.c_m = self.link.send(src, self.r2.at[1, 2:4], self.first(-1))

    def middle(self):
        for copy in (self.b_p, self.b_m, self.c_p, self.c_m):
            copy.wait_recv()
        for k in (2, 1, 3, 0):
            i = lax.rem(self.o + k, 4)
            at = self.index(0, i)
            self.s[i] = (
                self.full[at].astype(F32) + self.r2[0, i].astype(F32) + self.r2[1, i].astype(F32)
            ).astype(BF)
        p, q, m = (lax.rem(self.o + k, 4) for k in (1, 2, 3))
        self.d_p = self.link.send(self.s.at[q, 0:32], self.q1.at[0], self.second(1))
        self.d_m = self.link.send(self.s.at[q, 32:64], self.q1.at[1], self.second(-1))
        self.e_p = self.link.send(self.s.at[p, 32:64], self.q2.at[0, 32:64], self.second(1))
        self.e_m = self.link.send(self.s.at[m, 0:32], self.q2.at[1, 0:32], self.second(-1))

    def sums2(self):
        p, m = (lax.rem(self.o + k, 4) for k in (1, 3))
        self.d_p.wait_recv()
        self.s[p, 0:32] = (self.s[p, 0:32].astype(F32) + self.q1[0].astype(F32)).astype(BF)
        self.f_p = self.link.send(self.s.at[p, 0:32], self.q2.at[0, 0:32], self.second(1))
        self.d_m.wait_recv()
        self.s[m, 32:64] = (self.s[m, 32:64].astype(F32) + self.q1[1].astype(F32)).astype(BF)
        self.f_m = self.link.send(self.s.at[m, 32:64], self.q2.at[1, 32:64], self.second(-1))

    def arrive(self):
        for copy in (self.e_p, self.e_m, self.f_p, self.f_m):
            copy.wait_recv()

    def result(self, cols):
        return (
            self.s[self.o, :, cols].astype(F32)
            + self.q2[0, :, cols].astype(F32)
            + self.q2[1, :, cols].astype(F32)
        )


class GatherXY:
    def __init__(self, link, where, half, full):
        self.link, self.half, self.full = link, half, full
        if half == 0:
            self.m, self.o, self.first, self.second = where.x, where.y, where.X, where.Y
        else:
            self.m, self.o, self.first, self.second = where.y, where.x, where.Y, where.X
        self.p, self.q = [], []

    def at(self, k, j, *rows):
        a, b = lax.rem(self.m + k + 4, 4), lax.rem(self.o + j + 4, 4)
        return self.full.at[(a, b, self.half, *rows) if self.half == 0 else (b, a, self.half, *rows)]

    def send(self, ref, device):
        return self.link.send(ref, ref, device)

    def across(self, k):
        piece = self.at(k, 0)
        self.p.append(self.send(piece, self.second(1)))
        self.q.append(self.send(piece, self.second(-1)))

    def start(self):
        piece = self.at(0, 0)
        self.a_p = self.send(piece, self.first(1))
        self.a_m = self.send(piece, self.first(-1))
        self.across(0)

    def near(self):
        self.a_p.wait_recv()
        self.b_p = self.send(self.at(-1, 0, slice(0, 32)), self.first(1))
        self.a_m.wait_recv()
        self.b_m = self.send(self.at(1, 0, slice(32, 64)), self.first(-1))

    def far(self):
        self.b_p.wait_recv()
        self.b_m.wait_recv()

    def relay(self, n):
        k = (0, -1, 1, 2)[n]
        self.p[n].wait_recv()
        self.p[n] = self.send(self.at(k, -1, slice(0, 32)), self.second(1))
        self.q[n].wait_recv()
        self.q[n] = self.send(self.at(k, 1, slice(32, 64)), self.second(-1))

    def finish(self):
        for copy in self.p + self.q:
            copy.wait_recv()

    def group(self, j):
        b = lax.rem(self.o + j + 4, 4)
        return (slice(None), b, self.half) if self.half == 0 else (b, slice(None), self.half)


class ScatterZ:
    def __init__(self, link, where, full, side, right, left, out):
        self.link, self.w, self.full, self.side = link, where, full, side
        self.bufs, self.out = {1: right, -1: left}, out
        self.moves = {}

    def swap(self):
        other = 1 - self.w.core
        self.pair = [
            self.link.send(self.full.at[:, other + 2 * j], self.side.at[:, j], self.w.sibling)
            for j in range(2)
        ]

    def both(self, k, half):
        to = lax.rem(self.w.z + k + NZ, NZ)
        a, j = lax.div(to, 2), lax.rem(to, 2)
        at = (a, 2 * j + self.w.core, half)
        return at, self.full[at].astype(F32) + self.side[a, j, half].astype(F32)

    def move(self, way, n, half, arrived):
        at, total = self.both(way * (4 - n), half)
        if arrived:
            self.moves[way, half].wait_recv()
            total = total + self.bufs[way][n - 1, half].astype(F32)
        self.full[at] = total.astype(BF)
        self.moves[way, half] = self.link.send(self.full.at[at], self.bufs[way].at[n, half], self.w.Z(way))

    def begin(self):
        for copy in self.pair:
            copy.wait_recv()
        for way in (1, -1):
            self.move(way, 0, 0 if way == 1 else 1, False)
        for way in (1, -1):
            self.move(way, 1, 1 if way == 1 else 0, False)

    def step(self, n):
        for way in (1, -1):
            self.move(way, n, 0 if way == 1 else 1, True)
        if n < 3:
            for way in (1, -1):
                self.move(way, n + 1, 1 if way == 1 else 0, True)

    def finish(self):
        for half in range(2):
            total = self.both(0, half)[1]
            for way in (1, -1) if half == 1 else (-1, 1):
                self.moves[way, half].wait_recv()
                total = total + self.bufs[way][3, half].astype(F32)
            self.out[half] = total.astype(BF)


class Where:
    def __init__(self):
        r, c = lax.axis_index("row"), lax.axis_index("col")
        self.r, self.c = r, c
        self.x, self.y = lax.div(r, NY), lax.rem(r, NY)
        self.z, self.core = lax.div(c, 2), lax.rem(c, 2)
        self.sibling = (r, 2 * self.z + 1 - self.core)

    def X(self, k):
        return (lax.rem(self.x + k + NX, NX) * NY + self.y, self.c)

    def Y(self, k):
        return (self.x * NY + lax.rem(self.y + k + NY, NY), self.c)

    def Z(self, k):
        return (self.r, lax.rem(self.z + k + NZ, NZ) * 2 + self.core)


def kernel(
    tok, go, wg, wu, wd, gm, um, dm,
    lo, ig, gg, ug, dg,
    t_all, g_all, tt, gt, w, wdm, p_gu, p_hg,
    ra1, ra2, sa, qa1, qa2, rb1, rb2, sb, qb1, qb2,
    ha1, ha2, hsa, hqa1, hqa2, hb1, hb2, hsb, hqb1, hqb2,
    hid, gr, silu_s, slope_s, lop, igp, lo_side, ig_side, lo_r, lo_l, ig_r, ig_l,
    send_sem, recv_sem, load_sem,
):
    where = Where()
    link = Link(send_sem, recv_sem)

    loads = [
        pltpu.make_async_copy(wg, w.at[:, 0:F], load_sem.at[0]),
        pltpu.make_async_copy(wu, w.at[:, F : 2 * F], load_sem.at[1]),
        pltpu.make_async_copy(wd, wdm, load_sem.at[2]),
    ]
    for load in loads:
        load.start()

    barrier = pltpu.get_barrier_semaphore()
    near = (where.X(1), where.X(-1), where.Y(1), where.Y(-1), where.Z(1), where.Z(-1), where.sibling)
    for device in near:
        pl.semaphore_signal(barrier, inc=1, device_id=device, device_id_type=MESH)
    pl.semaphore_wait(barrier, len(near))

    tz = GatherZ(link, where, t_all, tok)
    gz = GatherZ(link, where, g_all, go)
    tz.start()

    for load in loads:
        load.wait()

    @pl.loop(0, 4)
    def _(i):
        rows = pl.ds(pl.multiple_of(i * BLK, BLK), BLK)
        for m_ref, base in ((gm, 0), (um, F)):
            for j in range(7):
                cols = pl.ds(base + j * BLK, BLK)
                w[rows, cols] = (w[rows, cols].astype(F32) * m_ref[i, j].astype(F32)).astype(BF)

    tz.step(1)

    @pl.loop(0, 7)
    def _(i):
        rows = pl.ds(pl.multiple_of(i * BLK, BLK), BLK)
        for j in range(4):
            cols = pl.ds(j * BLK, BLK)
            wdm[rows, cols] = (wdm[rows, cols].astype(F32) * dm[i, j].astype(F32)).astype(BF)

    tz.step(2)
    tz.step(3)
    gz.start()
    tz.last()
    tz.finish()

    gu = [
        ScatterXY(link, where, 0, p_gu, (ra1, ra2, sa, qa1, qa2)),
        ScatterXY(link, where, 1, p_gu, (rb1, rb2, sb, qb1, qb2)),
    ]
    hg = [
        ScatterXY(link, where, 0, p_hg, (ha1, ha2, hsa, hqa1, hqa2)),
        ScatterXY(link, where, 1, p_hg, (hb1, hb2, hsb, hqb1, hqb2)),
    ]

    def part_gu(s, k):
        at = s.index(k)

        @pl.loop(0, 2)
        def _(n):
            cols = pl.ds(pl.multiple_of(n * F, BLK), F)
            part = dot_nn(rows_of(t_all, *at), w[:, cols])
            p_gu[(*at, slice(None), cols)] = part.astype(BF).reshape(4, 64, F)

    def part_hg(s, k):
        at = s.index(k)
        p_hg[at] = dot_nt(rows_of(g_all, *at), wdm[...]).astype(BF).reshape(4, 64, F)

    def transpose(src, dst, first, last):
        @pl.loop(first, last)
        def _(c):
            block = src[lax.div(c, 4), lax.rem(c, 4)].reshape(BLK, D)
            dst[:, pl.ds(pl.multiple_of(c * BLK, BLK), BLK)] = block.T

    for s in gu:
        part_gu(s, 2)
        s.opposite()
    gz.step(1)
    for s in gu:
        part_gu(s, 1)
        part_gu(s, -1)
        s.raw()
    gz.step(2)
    part_gu(gu[0], 0)
    gz.step(3)
    part_gu(gu[1], 0)
    gz.last()
    gz.finish()
    for s in hg:
        part_hg(s, 2)
        s.opposite()
    for s in gu:
        s.sums()
    for s in hg:
        part_hg(s, 1)
        part_hg(s, -1)
        s.raw()
    for s in hg:
        part_hg(s, 0)
    transpose(t_all, tt, 0, 16)
    for s in hg:
        s.sums()
    for s in gu:
        s.middle()
    transpose(g_all, gt, 0, 16)
    for s in gu:
        s.sums2()
    for s in hg:
        s.middle()

    hid_ag = [GatherXY(link, where, h, hid) for h in range(2)]
    gr_ag = [GatherXY(link, where, h, gr) for h in range(2)]
    for h in range(2):
        gu[h].arrive()
        gate = gu[h].result(slice(0, F)).astype(BF).astype(F32)
        up = gu[h].result(slice(F, 2 * F)).astype(BF).astype(F32)
        sig = 1.0 / (1.0 + jnp.exp(-gate))
        silu = gate * sig
        silu_s[h] = silu
        slope_s[h] = up * (sig * (1.0 + gate * (1.0 - sig)))
        hid[where.x, where.y, h] = (silu * up).astype(BF)
        hid_ag[h].start()
    lz = ScatterZ(link, where, lop, lo_side, lo_r, lo_l, lo)
    iz = ScatterZ(link, where, igp, ig_side, ig_r, ig_l, ig)

    def out_part(a, first, last):
        @pl.loop(first, last)
        def _(j):
            at = (slice(None), j, a.half) if a.half == 0 else (j, slice(None), a.half)
            lop[at] = dot_nn(rows_of(hid, *at), wdm[...]).astype(BF).reshape(4, 64, D)

    def in_part(a, j):
        at = a.group(j)
        igp[at] = dot_nt(rows_of(gr, *at), w[...]).astype(BF).reshape(4, 64, D)

    def down_part(first, last):
        @pl.loop(first, last)
        def _(j):
            at = pl.ds(pl.multiple_of(j * BLK, BLK), BLK)

            @pl.loop(0, 7)
            def _(i):
                rows = pl.ds(pl.multiple_of(i * BLK, BLK), BLK)
                right = hid[:, :, :, :, rows].reshape(2048, BLK)
                part = dot_nn(gt[at, :], right) * dm[i, j].astype(F32)
                dg[rows, at] = part.T.astype(BF)

    for s in hg:
        s.sums2()
    for a in hid_ag:
        a.near()
    for a in hid_ag:
        a.across(-1)
        a.across(1)
    for h in range(2):
        hg[h].arrive()
        hgrad = hg[h].result(slice(0, F))
        gr[where.x, where.y, h, :, 0:F] = (hgrad * slope_s[h]).astype(BF)
        gr[where.x, where.y, h, :, F : 2 * F] = (hgrad * silu_s[h]).astype(BF)
        gr_ag[h].start()
    for a in hid_ag:
        a.far()
        a.across(2)
    for n in range(3):
        for a in hid_ag:
            a.relay(n)
    for a in gr_ag:
        a.near()
    for a in hid_ag:
        a.relay(3)
    for a in gr_ag:
        a.across(-1)
        a.across(1)
    for a in gr_ag:
        a.far()
        a.across(2)
    for a in hid_ag:
        a.finish()
    for a in hid_ag:
        out_part(a, 0, 4)
    lz.swap()
    for a in gr_ag:
        a.relay(0)
    lz.begin()
    for a in gr_ag:
        in_part(a, 0)
    for a in gr_ag:
        a.relay(1)
    lz.step(1)
    down_part(0, 1)
    for a in gr_ag:
        a.relay(2)
    lz.step(2)
    down_part(1, 2)
    for a in gr_ag:
        a.relay(3)
    lz.step(3)
    down_part(2, 4)
    lz.finish()
    for a in gr_ag:
        a.finish()
    for a in gr_ag:
        in_part(a, -1)
        in_part(a, 1)
        in_part(a, 2)
    iz.swap()

    def weight_part(m_ref, out, base, first, last):
        @pl.loop(first, last)
        def _(j):
            cols = pl.ds(pl.multiple_of(base + j * BLK, BLK), BLK)
            right = gr[:, :, :, :, cols].reshape(2048, BLK)
            part = dot_nn(tt[...], right)
            at = pl.ds(pl.multiple_of(j * BLK, BLK), BLK)
            for i in range(4):
                rows = slice(i * BLK, (i + 1) * BLK)
                out[rows, at] = (part[rows] * m_ref[i, j].astype(F32)).astype(BF)

    iz.begin()
    weight_part(gm, gg, 0, 0, 4)
    iz.step(1)
    weight_part(gm, gg, 0, 4, 7)
    iz.step(2)
    weight_part(um, ug, F, 0, 4)
    iz.step(3)
    weight_part(um, ug, F, 4, 7)
    iz.finish()
    link.drain()


def scatter_bufs(n):
    return [
        pltpu.VMEM((2, 2, 64, n), BF),
        pltpu.VMEM((2, 4, 64, n), BF),
        pltpu.VMEM((4, 64, n), BF),
        pltpu.VMEM((2, 32, n), BF),
        pltpu.VMEM((2, 64, n), BF),
    ]


def body(tokens, grad_out, gate_weight, up_weight, down_weight, gate_mask, up_mask, down_mask):
    vmem = pl.BlockSpec(memory_space=pltpu.VMEM)
    smem = pl.BlockSpec(memory_space=pltpu.SMEM)
    anywhere = pl.BlockSpec(memory_space=pl.ANY)
    chunks = (4, 4, 2, 64)
    lo, ig, gg, ug, dg = pl.pallas_call(
        kernel,
        out_shape=(
            jax.ShapeDtypeStruct((2, 64, D), BF),
            jax.ShapeDtypeStruct((2, 64, D), BF),
            jax.ShapeDtypeStruct((D, F), BF),
            jax.ShapeDtypeStruct((D, F), BF),
            jax.ShapeDtypeStruct((F, D), BF),
        ),
        in_specs=[vmem, vmem, anywhere, anywhere, anywhere, smem, smem, smem],
        out_specs=(vmem,) * 5,
        scratch_shapes=[
            pltpu.VMEM((*chunks, D), BF),
            pltpu.VMEM((*chunks, D), BF),
            pltpu.VMEM((D, 2048), BF),
            pltpu.VMEM((D, 2048), BF),
            pltpu.VMEM((D, 2 * F), BF),
            pltpu.VMEM((F, D), BF),
            pltpu.VMEM((*chunks, 2 * F), BF),
            pltpu.VMEM((*chunks, F), BF),
            *scatter_bufs(2 * F), *scatter_bufs(2 * F),
            *scatter_bufs(F), *scatter_bufs(F),
            pltpu.VMEM((*chunks, F), BF),
            pltpu.VMEM((*chunks, 2 * F), BF),
            pltpu.VMEM((2, 64, F), F32),
            pltpu.VMEM((2, 64, F), F32),
            pltpu.VMEM((*chunks, D), BF),
            pltpu.VMEM((*chunks, D), BF),
            pltpu.VMEM((4, 2, 2, 64, D), BF),
            pltpu.VMEM((4, 2, 2, 64, D), BF),
            *[pltpu.VMEM((4, 2, 64, D), BF)] * 4,
            pltpu.SemaphoreType.DMA((NSEM,)),
            pltpu.SemaphoreType.DMA((NSEM,)),
            pltpu.SemaphoreType.DMA((3,)),
        ],
        compiler_params=pltpu.CompilerParams(
            collective_id=0, has_side_effects=True, vmem_limit_bytes=63 * 2**20
        ),
        cost_estimate=pl.CostEstimate(flops=2 * 9 * 2048 * D * F, bytes_accessed=8 * 2**20, transcendentals=0),
    )(
        tokens.reshape(2, 64, D), grad_out.reshape(2, 64, D), gate_weight, up_weight, down_weight,
        gate_mask, up_mask, down_mask,
    )
    return lo.reshape(BLK, D), ig.reshape(BLK, D), gg, ug, dg


def solution(mesh):
    wide, tall = P("row", "col"), P("col", "row")
    return jax.shard_map(
        body,
        mesh=mesh,
        in_specs=(tall, tall, wide, wide, tall, wide, wide, tall),
        out_specs=(tall, tall, wide, wide, tall),
        check_vma=False,
    )
```

```python
import jax
import jax.numpy as jnp
from jax import lax
from jax.experimental import pallas as pl
from jax.experimental.pallas import tpu as pltpu
from jax.sharding import PartitionSpec as P

BLK = 128
NX, NY, NZ = 4, 4, 8
F = 896
D = 512
F32, BF = jnp.float32, jnp.bfloat16
MESH = pl.DeviceIdType.MESH
NSEM = 240


def rows_of(ref, *lead):
    value = ref[lead]
    return value.reshape(256, value.shape[-1])


def dot_nn(a, b):
    return jnp.dot(a, b, preferred_element_type=F32)


def dot_nt(a, b):
    return lax.dot_general(a, b, (((1,), (1,)), ((), ())), preferred_element_type=F32)


class Link:
    def __init__(self, send_sem, recv_sem):
        self.send_sem, self.recv_sem, self.copies = send_sem, recv_sem, []

    def prepare(self, src, dst, device):
        at = len(self.copies)
        copy = pltpu.make_async_remote_copy(
            src_ref=src, dst_ref=dst, send_sem=self.send_sem.at[at], recv_sem=self.recv_sem.at[at],
            device_id=device, device_id_type=MESH,
        )
        self.copies.append(copy)
        return copy

    def send(self, src, dst, device):
        copy = self.prepare(src, dst, device)
        copy.start()
        return copy

    def drain(self):
        for copy in self.copies:
            copy.wait_send()


class GatherZ:
    def __init__(self, link, where, full, own):
        self.link, self.w, self.full, self.own = link, where, full, own
        self.moves = {}

    def slot(self, k, *half):
        chunk = lax.rem(self.w.z + k + NZ, NZ) * 2 + self.w.core
        return self.full.at[(lax.div(chunk, 4), lax.rem(chunk, 4), *half)]

    def move(self, way, k, half):
        ref = self.slot(k, half)
        self.moves[way, half] = self.link.send(ref, ref, self.w.Z(way))

    def start(self):
        own = self.slot(0)
        own[...] = self.own[...]
        for half in range(2):
            for way in (1, -1):
                self.move(way, 0, half if way == 1 else 1 - half)
        self.side = [self.link.send(own, own, self.w.sibling)]

    def step(self, k):
        for turn in range(2):
            for way in (1, -1):
                half = turn if way == 1 else 1 - turn
                self.moves[way, half].wait_recv()
                if k < 3 or turn == 0:
                    self.move(way, -way * k, half)
        for way in (1, -1):
            got = self.slot(-way * k)
            self.side.append(self.link.send(got, got, self.w.sibling))

    def last(self):
        self.moves[1, 0].wait_recv()
        self.moves[-1, 1].wait_recv()
        got = self.slot(4)
        self.side.append(self.link.send(got, got, self.w.sibling))

    def ready(self, first, last):
        for copy in self.side[first:last]:
            copy.wait_recv()


class ScatterXY:
    def __init__(self, link, where, half, full, bufs):
        self.link, self.half, self.full = link, half, full
        self.r1, self.r2, self.s, self.q1, self.q2 = bufs
        self.m, self.o, self.first, self.second = where.order(half)
        lo, hi = slice(0, 2), slice(2, 4)
        prepare = self.link.prepare
        self.far = [
            prepare(self.part(2, lo), self.r1.at[0], self.first(1)),
            prepare(self.part(2, hi), self.r1.at[1], self.first(-1)),
        ]
        self.plain = [
            prepare(self.part(1, hi), self.r2.at[0, hi], self.first(1)),
            prepare(self.part(-1, lo), self.r2.at[1, lo], self.first(-1)),
        ]
        self.summed = [
            prepare(self.part(1, lo), self.r2.at[0, lo], self.first(1)),
            prepare(self.part(-1, hi), self.r2.at[1, hi], self.first(-1)),
        ]

    def index(self, k, o):
        return (lax.rem(self.m + k + 4, 4), o, self.half)

    def part(self, k, o):
        return self.full.at[self.index(k, o)]

    def launch(self, group):
        away = lax.rem(group - self.m + 4, 4)

        @pl.when(away == 2)
        def _():
            for copy in self.far:
                copy.start()

        for i, k in ((0, 1), (1, 3)):

            @pl.when(away == k)
            def _():
                self.plain[i].start()

    def sums(self, group):
        away = lax.rem(group - self.m + 4, 4)
        for i, k, o in ((0, 1, 0), (1, 3, 2)):

            @pl.when(away == k)
            def _():
                self.far[i].wait_recv()
                for j in range(2):
                    at = self.index(k, o + j)
                    self.full[at] = (self.full[at].astype(F32) + self.r1[i, j].astype(F32)).astype(BF)
                self.summed[i].start()

    def middle(self):
        for copy in self.plain + self.summed:
            copy.wait_recv()
        for k in (2, 1, 3, 0):
            i = lax.rem(self.o + k, 4)
            at = self.index(0, i)
            self.s[i] = (
                self.full[at].astype(F32) + self.r2[0, i].astype(F32) + self.r2[1, i].astype(F32)
            ).astype(BF)
        p, q, m = (lax.rem(self.o + k, 4) for k in (1, 2, 3))
        self.d_p = self.link.send(self.s.at[q, 0:32], self.q1.at[0], self.second(1))
        self.d_m = self.link.send(self.s.at[q, 32:64], self.q1.at[1], self.second(-1))
        self.e_p = self.link.send(self.s.at[p, 32:64], self.q2.at[0, 32:64], self.second(1))
        self.e_m = self.link.send(self.s.at[m, 0:32], self.q2.at[1, 0:32], self.second(-1))

    def sums2(self):
        p, m = (lax.rem(self.o + k, 4) for k in (1, 3))
        self.d_p.wait_recv()
        self.s[p, 0:32] = (self.s[p, 0:32].astype(F32) + self.q1[0].astype(F32)).astype(BF)
        self.f_p = self.link.send(self.s.at[p, 0:32], self.q2.at[0, 0:32], self.second(1))
        self.d_m.wait_recv()
        self.s[m, 32:64] = (self.s[m, 32:64].astype(F32) + self.q1[1].astype(F32)).astype(BF)
        self.f_m = self.link.send(self.s.at[m, 32:64], self.q2.at[1, 32:64], self.second(-1))

    def arrive(self):
        for copy in (self.e_p, self.e_m, self.f_p, self.f_m):
            copy.wait_recv()

    def result(self, cols):
        return (
            self.s[self.o, :, cols].astype(F32)
            + self.q2[0, :, cols].astype(F32)
            + self.q2[1, :, cols].astype(F32)
        )


class GatherXY:
    def __init__(self, link, where, half, full):
        self.link, self.half, self.full = link, half, full
        self.m, self.o, self.first, self.second = where.order(half)
        self.p, self.q = [], []

    def at(self, k, j, *rows):
        a, b = lax.rem(self.m + k + 4, 4), lax.rem(self.o + j + 4, 4)
        return self.full.at[(a, b, self.half, *rows)]

    def send(self, ref, device):
        return self.link.send(ref, ref, device)

    def across(self, k):
        piece = self.at(k, 0)
        self.p.append(self.send(piece, self.second(1)))
        self.q.append(self.send(piece, self.second(-1)))

    def start(self):
        piece = self.at(0, 0)
        self.a_p = self.send(piece, self.first(1))
        self.a_m = self.send(piece, self.first(-1))
        self.across(0)

    def near(self):
        self.a_p.wait_recv()
        self.b_p = self.send(self.at(-1, 0, slice(0, 32)), self.first(1))
        self.a_m.wait_recv()
        self.b_m = self.send(self.at(1, 0, slice(32, 64)), self.first(-1))

    def far(self):
        self.b_p.wait_recv()
        self.b_m.wait_recv()

    def relay(self, n):
        k = (0, -1, 1, 2)[n]
        self.p[n].wait_recv()
        self.p[n] = self.send(self.at(k, -1, slice(0, 32)), self.second(1))
        self.q[n].wait_recv()
        self.q[n] = self.send(self.at(k, 1, slice(32, 64)), self.second(-1))

    def finish(self):
        for copy in self.p + self.q:
            copy.wait_recv()

    def group(self, j):
        return (slice(None), lax.rem(self.o + j + 4, 4), self.half)


class ScatterZ:
    def __init__(self, link, where, full, side, right, left, out):
        self.link, self.w, self.full, self.side = link, where, full, side
        self.bufs, self.out = {1: right, -1: left}, out
        self.moves = {}

    def swap(self):
        other = 1 - self.w.core
        self.pair = [
            self.link.send(self.full.at[:, other + 2 * j], self.side.at[:, j], self.w.sibling)
            for j in range(2)
        ]

    def both(self, k, half):
        to = lax.rem(self.w.z + k + NZ, NZ)
        a, j = lax.div(to, 2), lax.rem(to, 2)
        at = (a, 2 * j + self.w.core, half)
        return at, self.full[at].astype(F32) + self.side[a, j, half].astype(F32)

    def move(self, way, n, half, arrived):
        at, total = self.both(way * (4 - n), half)
        if arrived:
            self.moves[way, half].wait_recv()
            total = total + self.bufs[way][n - 1, half].astype(F32)
        self.full[at] = total.astype(BF)
        self.moves[way, half] = self.link.send(self.full.at[at], self.bufs[way].at[n, half], self.w.Z(way))

    def begin(self):
        for copy in self.pair:
            copy.wait_recv()
        for way in (1, -1):
            self.move(way, 0, 0 if way == 1 else 1, False)
        for way in (1, -1):
            self.move(way, 1, 1 if way == 1 else 0, False)

    def step(self, n):
        for way in (1, -1):
            self.move(way, n, 0 if way == 1 else 1, True)
        if n < 3:
            for way in (1, -1):
                self.move(way, n + 1, 1 if way == 1 else 0, True)

    def finish(self):
        for half in range(2):
            total = self.both(0, half)[1]
            for way in (1, -1) if half == 1 else (-1, 1):
                self.moves[way, half].wait_recv()
                total = total + self.bufs[way][3, half].astype(F32)
            self.out[half] = total.astype(BF)


class Where:
    def __init__(self):
        r, c = lax.axis_index("row"), lax.axis_index("col")
        self.r, self.c = r, c
        self.x, self.y = lax.div(r, NY), lax.rem(r, NY)
        self.z, self.core = lax.div(c, 2), lax.rem(c, 2)
        self.sibling = (r, 2 * self.z + 1 - self.core)
        near, toward = lax.div(self.z, 2), 1 - 2 * lax.rem(self.z, 2)
        self.groups = [lax.rem(near + k + 4, 4) for k in (0, -toward, toward, 2)]

    def order(self, half):
        return (self.x, self.y, self.X, self.Y) if half == 0 else (self.y, self.x, self.Y, self.X)

    def X(self, k):
        return (lax.rem(self.x + k + NX, NX) * NY + self.y, self.c)

    def Y(self, k):
        return (self.x * NY + lax.rem(self.y + k + NY, NY), self.c)

    def Z(self, k):
        return (self.r, lax.rem(self.z + k + NZ, NZ) * 2 + self.core)


def kernel(
    tok, go, wg, wu, wd, gm, um, dm,
    lo, ig, gg, ug, dg,
    t_all, g_all, tt, gt, w, wdm, p_gu, p_hg,
    ra1, ra2, sa, qa1, qa2, rb1, rb2, sb, qb1, qb2,
    ha1, ha2, hsa, hqa1, hqa2, hb1, hb2, hsb, hqb1, hqb2,
    hid, gr, silu_s, slope_s, lop, igp, lo_side, ig_side, lo_r, lo_l, ig_r, ig_l,
    send_sem, recv_sem, load_sem,
):
    where = Where()
    link = Link(send_sem, recv_sem)

    loads = [
        pltpu.make_async_copy(wg, w.at[:, 0:F], load_sem.at[0]),
        pltpu.make_async_copy(wu, w.at[:, F : 2 * F], load_sem.at[1]),
        pltpu.make_async_copy(wd, wdm, load_sem.at[2]),
    ]
    for load in loads:
        load.start()

    barrier = pltpu.get_barrier_semaphore()
    near = (where.X(1), where.X(-1), where.Y(1), where.Y(-1), where.Z(1), where.Z(-1), where.sibling)
    for device in near:
        pl.semaphore_signal(barrier, inc=1, device_id=device, device_id_type=MESH)
    pl.semaphore_wait(barrier, len(near))

    tz = GatherZ(link, where, t_all, tok)
    gz = GatherZ(link, where, g_all, go)
    tz.start()

    for load in loads:
        load.wait()

    @pl.loop(0, 4)
    def _(i):
        rows = pl.ds(pl.multiple_of(i * BLK, BLK), BLK)
        for m_ref, base in ((gm, 0), (um, F)):
            for j in range(7):
                cols = pl.ds(base + j * BLK, BLK)
                w[rows, cols] = (w[rows, cols].astype(F32) * m_ref[i, j].astype(F32)).astype(BF)

    gu = [
        ScatterXY(link, where, 0, p_gu, (ra1, ra2, sa, qa1, qa2)),
        ScatterXY(link, where, 1, p_gu, (rb1, rb2, sb, qb1, qb2)),
    ]
    hg = [
        ScatterXY(link, where, 0, p_hg, (ha1, ha2, hsa, hqa1, hqa2)),
        ScatterXY(link, where, 1, p_hg, (hb1, hb2, hsb, hqb1, hqb2)),
    ]

    def part_gu(n):
        g = where.groups[n]

        @pl.loop(0, 2)
        def _(n):
            cols = pl.ds(pl.multiple_of(n * F, BLK), F)
            part = dot_nn(t_all[g].reshape(512, D), w[:, cols])
            p_gu[g, :, :, :, cols] = part.astype(BF).reshape(4, 2, 64, F)

        for s in gu:
            s.launch(g)

    def part_hg(n):
        g = where.groups[n]
        p_hg[g] = dot_nt(g_all[g].reshape(512, D), wdm[...]).astype(BF).reshape(4, 2, 64, F)
        for s in hg:
            s.launch(g)

    def sums(scatter, n):
        for s in scatter:
            s.sums(where.groups[n])

    def transpose(src, dst, first, last):
        @pl.loop(first, last)
        def _(c):
            block = src[lax.div(c, 4), lax.rem(c, 4)].reshape(BLK, D)
            dst[:, pl.ds(pl.multiple_of(c * BLK, BLK), BLK)] = block.T

    tz.step(1)
    tz.ready(0, 3)
    part_gu(0)
    tz.step(2)
    tz.ready(3, 5)
    part_gu(1)
    tz.step(3)
    gz.start()
    tz.ready(5, 7)
    part_gu(2)
    tz.last()
    tz.ready(7, 8)
    part_gu(3)

    @pl.loop(0, 7)
    def _(i):
        rows = pl.ds(pl.multiple_of(i * BLK, BLK), BLK)
        for j in range(4):
            cols = pl.ds(j * BLK, BLK)
            wdm[rows, cols] = (wdm[rows, cols].astype(F32) * dm[i, j].astype(F32)).astype(BF)

    gz.step(1)
    sums(gu, 0)
    gz.step(2)
    gz.ready(0, 3)
    part_hg(0)
    sums(gu, 1)
    gz.step(3)
    gz.ready(3, 5)
    part_hg(1)
    sums(gu, 2)
    gz.last()
    gz.ready(5, 8)
    part_hg(2)
    part_hg(3)
    sums(gu, 3)
    transpose(t_all, tt, 0, 16)
    for n in range(4):
        sums(hg, n)
    for s in gu:
        s.middle()
    transpose(g_all, gt, 0, 16)
    for s in gu:
        s.sums2()
    for s in hg:
        s.middle()

    hid_ag = [GatherXY(link, where, h, hid) for h in range(2)]
    gr_ag = [GatherXY(link, where, h, gr) for h in range(2)]
    for h in range(2):
        gu[h].arrive()
        gate = gu[h].result(slice(0, F)).astype(BF).astype(F32)
        up = gu[h].result(slice(F, 2 * F)).astype(BF).astype(F32)
        sig = 1.0 / (1.0 + jnp.exp(-gate))
        silu = gate * sig
        silu_s[h] = silu
        slope_s[h] = up * (sig * (1.0 + gate * (1.0 - sig)))
        hid[hid_ag[h].m, hid_ag[h].o, h] = (silu * up).astype(BF)
        hid_ag[h].start()
    lz = ScatterZ(link, where, lop, lo_side, lo_r, lo_l, lo)
    iz = ScatterZ(link, where, igp, ig_side, ig_r, ig_l, ig)

    def out_part(a, first, last):
        @pl.loop(first, last)
        def _(j):
            at = (slice(None), j, a.half)
            lop[at] = dot_nn(rows_of(hid, *at), wdm[...]).astype(BF).reshape(4, 64, D)

    def in_part(a, j):
        at = a.group(j)
        igp[at] = dot_nt(rows_of(gr, *at), w[...]).astype(BF).reshape(4, 64, D)

    def down_part(first, last):
        @pl.loop(first, last)
        def _(j):
            at = pl.ds(pl.multiple_of(j * BLK, BLK), BLK)

            @pl.loop(0, 7)
            def _(i):
                rows = pl.ds(pl.multiple_of(i * BLK, BLK), BLK)
                right = hid[:, :, :, :, rows].reshape(2048, BLK)
                part = dot_nn(gt[at, :], right) * dm[i, j].astype(F32)
                dg[rows, at] = part.T.astype(BF)

    for s in hg:
        s.sums2()
    for a in hid_ag:
        a.near()
    for a in hid_ag:
        a.across(-1)
        a.across(1)
    for h in range(2):
        hg[h].arrive()
        hgrad = hg[h].result(slice(0, F))
        gr[gr_ag[h].m, gr_ag[h].o, h, :, 0:F] = (hgrad * slope_s[h]).astype(BF)
        gr[gr_ag[h].m, gr_ag[h].o, h, :, F : 2 * F] = (hgrad * silu_s[h]).astype(BF)
        gr_ag[h].start()
    for a in hid_ag:
        a.far()
        a.across(2)
    for n in range(3):
        for a in hid_ag:
            a.relay(n)
    for a in gr_ag:
        a.near()
    for a in hid_ag:
        a.relay(3)
    for a in gr_ag:
        a.across(-1)
        a.across(1)
    for a in gr_ag:
        a.far()
        a.across(2)
    for a in hid_ag:
        a.finish()
    for a in hid_ag:
        out_part(a, 0, 4)
    lz.swap()
    for a in gr_ag:
        a.relay(0)
    lz.begin()
    for a in gr_ag:
        in_part(a, 0)
    for a in gr_ag:
        a.relay(1)
    lz.step(1)
    down_part(0, 1)
    for a in gr_ag:
        a.relay(2)
    lz.step(2)
    down_part(1, 2)
    for a in gr_ag:
        a.relay(3)
    lz.step(3)
    down_part(2, 4)
    lz.finish()
    for a in gr_ag:
        a.finish()
    for a in gr_ag:
        in_part(a, -1)
        in_part(a, 1)
        in_part(a, 2)
    iz.swap()

    def weight_part(m_ref, out, base, first, last):
        @pl.loop(first, last)
        def _(j):
            cols = pl.ds(pl.multiple_of(base + j * BLK, BLK), BLK)
            right = gr[:, :, :, :, cols].reshape(2048, BLK)
            part = dot_nn(tt[...], right)
            at = pl.ds(pl.multiple_of(j * BLK, BLK), BLK)
            for i in range(4):
                rows = slice(i * BLK, (i + 1) * BLK)
                out[rows, at] = (part[rows] * m_ref[i, j].astype(F32)).astype(BF)

    iz.begin()
    weight_part(gm, gg, 0, 0, 4)
    iz.step(1)
    weight_part(gm, gg, 0, 4, 7)
    iz.step(2)
    weight_part(um, ug, F, 0, 4)
    iz.step(3)
    weight_part(um, ug, F, 4, 7)
    iz.finish()
    link.drain()


def scatter_bufs(n):
    return [
        pltpu.VMEM((2, 2, 64, n), BF),
        pltpu.VMEM((2, 4, 64, n), BF),
        pltpu.VMEM((4, 64, n), BF),
        pltpu.VMEM((2, 32, n), BF),
        pltpu.VMEM((2, 64, n), BF),
    ]


def hand_over(*refs):
    sems = refs[-1]
    copies = [pltpu.make_async_copy(refs[i], refs[i + 5], sems.at[i]) for i in range(5)]
    for copy in copies:
        copy.start()
    for copy in copies:
        copy.wait()


def body(tokens, grad_out, gate_weight, up_weight, down_weight, gate_mask, up_mask, down_mask):
    vmem = pl.BlockSpec(memory_space=pltpu.VMEM)
    smem = pl.BlockSpec(memory_space=pltpu.SMEM)
    anywhere = pl.BlockSpec(memory_space=pl.ANY)
    chunks = (4, 4, 2, 64)
    lo, ig, gg, ug, dg = pl.pallas_call(
        kernel,
        out_shape=(
            jax.ShapeDtypeStruct((2, 64, D), BF),
            jax.ShapeDtypeStruct((2, 64, D), BF),
            jax.ShapeDtypeStruct((D, F), BF),
            jax.ShapeDtypeStruct((D, F), BF),
            jax.ShapeDtypeStruct((F, D), BF),
        ),
        in_specs=[vmem, vmem, anywhere, anywhere, anywhere, smem, smem, smem],
        out_specs=(vmem,) * 5,
        scratch_shapes=[
            pltpu.VMEM((*chunks, D), BF),
            pltpu.VMEM((*chunks, D), BF),
            pltpu.VMEM((D, 2048), BF),
            pltpu.VMEM((D, 2048), BF),
            pltpu.VMEM((D, 2 * F), BF),
            pltpu.VMEM((F, D), BF),
            pltpu.VMEM((*chunks, 2 * F), BF),
            pltpu.VMEM((*chunks, F), BF),
            *scatter_bufs(2 * F), *scatter_bufs(2 * F),
            *scatter_bufs(F), *scatter_bufs(F),
            pltpu.VMEM((*chunks, F), BF),
            pltpu.VMEM((*chunks, 2 * F), BF),
            pltpu.VMEM((2, 64, F), F32),
            pltpu.VMEM((2, 64, F), F32),
            pltpu.VMEM((*chunks, D), BF),
            pltpu.VMEM((*chunks, D), BF),
            pltpu.VMEM((4, 2, 2, 64, D), BF),
            pltpu.VMEM((4, 2, 2, 64, D), BF),
            *[pltpu.VMEM((4, 2, 64, D), BF)] * 4,
            pltpu.SemaphoreType.DMA((NSEM,)),
            pltpu.SemaphoreType.DMA((NSEM,)),
            pltpu.SemaphoreType.DMA((3,)),
        ],
        compiler_params=pltpu.CompilerParams(
            collective_id=0, has_side_effects=True, vmem_limit_bytes=63 * 2**20
        ),
        cost_estimate=pl.CostEstimate(flops=2 * 9 * 2048 * D * F, bytes_accessed=8 * 2**20, transcendentals=0),
    )(
        tokens.reshape(2, 64, D), grad_out.reshape(2, 64, D), gate_weight, up_weight, down_weight,
        gate_mask, up_mask, down_mask,
    )
    hbm = pl.BlockSpec(memory_space=pltpu.HBM)
    results = (lo.reshape(BLK, D), ig.reshape(BLK, D), gg, ug, dg)
    return pl.pallas_call(
        hand_over,
        out_shape=tuple(jax.ShapeDtypeStruct(r.shape, r.dtype) for r in results),
        in_specs=[hbm] * 5,
        out_specs=(hbm,) * 5,
        scratch_shapes=[pltpu.SemaphoreType.DMA((5,))],
        compiler_params=pltpu.CompilerParams(vmem_limit_bytes=63 * 2**20),
    )(*results)


def solution(mesh):
    wide, tall = P("row", "col"), P("col", "row")
    return jax.shard_map(
        body,
        mesh=mesh,
        in_specs=(tall, tall, wide, wide, tall, wide, wide, tall),
        out_specs=(tall, tall, wide, wide, tall),
        check_vma=False,
    )
```

```python
import jax
import jax.numpy as jnp
from jax import lax
from jax.experimental import pallas as pl
from jax.experimental.pallas import tpu as pltpu
from jax.sharding import PartitionSpec as P

BLK = 128
NX, NY, NZ = 4, 4, 8
F = 896
D = 512
F32, BF = jnp.float32, jnp.bfloat16
MESH = pl.DeviceIdType.MESH
NSEM = 240


def rows_of(ref, *lead):
    value = ref[lead]
    return value.reshape(256, value.shape[-1])


def dot_nn(a, b):
    return jnp.dot(a, b, preferred_element_type=F32)


def dot_nt(a, b):
    return lax.dot_general(a, b, (((1,), (1,)), ((), ())), preferred_element_type=F32)


class Link:
    def __init__(self, send_sem, recv_sem):
        self.send_sem, self.recv_sem, self.copies = send_sem, recv_sem, []

    def prepare(self, src, dst, device):
        at = len(self.copies)
        copy = pltpu.make_async_remote_copy(
            src_ref=src, dst_ref=dst, send_sem=self.send_sem.at[at], recv_sem=self.recv_sem.at[at],
            device_id=device, device_id_type=MESH,
        )
        self.copies.append(copy)
        return copy

    def send(self, src, dst, device):
        copy = self.prepare(src, dst, device)
        copy.start()
        return copy

    def drain(self):
        for copy in self.copies:
            copy.wait_send()


class GatherZ:
    def __init__(self, link, where, full, own):
        self.link, self.w, self.full, self.own = link, where, full, own
        self.moves = {}

    def slot(self, k, *half):
        chunk = lax.rem(self.w.z + k + NZ, NZ) * 2 + self.w.core
        return self.full.at[(lax.div(chunk, 4), lax.rem(chunk, 4), *half)]

    def move(self, way, k, half):
        ref = self.slot(k, half)
        self.moves[way, half] = self.link.send(ref, ref, self.w.Z(way))

    def start(self):
        own = self.slot(0)
        own[...] = self.own[...]
        for half in range(2):
            for way in (1, -1):
                self.move(way, 0, half if way == 1 else 1 - half)
        self.side = [self.link.send(own, own, self.w.sibling)]

    def step(self, k):
        for turn in range(2):
            for way in (1, -1):
                half = turn if way == 1 else 1 - turn
                self.moves[way, half].wait_recv()
                if k < 3 or turn == 0:
                    self.move(way, -way * k, half)
        for way in (1, -1):
            got = self.slot(-way * k)
            self.side.append(self.link.send(got, got, self.w.sibling))

    def last(self):
        self.moves[1, 0].wait_recv()
        self.moves[-1, 1].wait_recv()
        got = self.slot(4)
        self.side.append(self.link.send(got, got, self.w.sibling))

    def ready(self, first, last):
        for copy in self.side[first:last]:
            copy.wait_recv()


class ScatterXY:
    def __init__(self, link, where, half, full, bufs):
        self.link, self.half, self.full = link, half, full
        self.r1, self.r2, self.s, self.q1, self.q2 = bufs
        self.m, self.o, self.first, self.second = where.order(half)
        lo, hi = slice(0, 2), slice(2, 4)
        prepare = self.link.prepare
        self.far = [
            prepare(self.part(2, lo), self.r1.at[0], self.first(1)),
            prepare(self.part(2, hi), self.r1.at[1], self.first(-1)),
        ]
        self.plain = [
            prepare(self.part(1, hi), self.r2.at[0, hi], self.first(1)),
            prepare(self.part(-1, lo), self.r2.at[1, lo], self.first(-1)),
        ]
        self.summed = [
            prepare(self.part(1, lo), self.r2.at[0, lo], self.first(1)),
            prepare(self.part(-1, hi), self.r2.at[1, hi], self.first(-1)),
        ]

    def index(self, k, o):
        return (lax.rem(self.m + k + 4, 4), o, self.half)

    def part(self, k, o):
        return self.full.at[self.index(k, o)]

    def launch(self, group):
        away = lax.rem(group - self.m + 4, 4)

        @pl.when(away == 2)
        def _():
            for copy in self.far:
                copy.start()

        for i, k in ((0, 1), (1, 3)):

            @pl.when(away == k)
            def _():
                self.plain[i].start()

    def sums(self, group):
        away = lax.rem(group - self.m + 4, 4)
        for i, k, o in ((0, 1, 0), (1, 3, 2)):

            @pl.when(away == k)
            def _():
                self.far[i].wait_recv()
                for j in range(2):
                    at = self.index(k, o + j)
                    self.full[at] = (self.full[at].astype(F32) + self.r1[i, j].astype(F32)).astype(BF)
                self.summed[i].start()

    def middle(self):
        for copy in self.plain + self.summed:
            copy.wait_recv()
        for k in (2, 1, 3, 0):
            i = lax.rem(self.o + k, 4)
            at = self.index(0, i)
            self.s[i] = (
                self.full[at].astype(F32) + self.r2[0, i].astype(F32) + self.r2[1, i].astype(F32)
            ).astype(BF)
        p, q, m = (lax.rem(self.o + k, 4) for k in (1, 2, 3))
        self.d_p = self.link.send(self.s.at[q, 0:32], self.q1.at[0], self.second(1))
        self.d_m = self.link.send(self.s.at[q, 32:64], self.q1.at[1], self.second(-1))
        self.e_p = self.link.send(self.s.at[p, 32:64], self.q2.at[0, 32:64], self.second(1))
        self.e_m = self.link.send(self.s.at[m, 0:32], self.q2.at[1, 0:32], self.second(-1))

    def sums2(self):
        p, m = (lax.rem(self.o + k, 4) for k in (1, 3))
        self.d_p.wait_recv()
        self.s[p, 0:32] = (self.s[p, 0:32].astype(F32) + self.q1[0].astype(F32)).astype(BF)
        self.f_p = self.link.send(self.s.at[p, 0:32], self.q2.at[0, 0:32], self.second(1))
        self.d_m.wait_recv()
        self.s[m, 32:64] = (self.s[m, 32:64].astype(F32) + self.q1[1].astype(F32)).astype(BF)
        self.f_m = self.link.send(self.s.at[m, 32:64], self.q2.at[1, 32:64], self.second(-1))

    def arrive(self):
        for copy in (self.e_p, self.e_m, self.f_p, self.f_m):
            copy.wait_recv()

    def result(self, cols):
        return (
            self.s[self.o, :, cols].astype(F32)
            + self.q2[0, :, cols].astype(F32)
            + self.q2[1, :, cols].astype(F32)
        )


class GatherXY:
    def __init__(self, link, where, half, full):
        self.link, self.half, self.full = link, half, full
        self.m, self.o, self.first, self.second = where.order(half)
        self.p, self.q = [], []

    def at(self, k, j, *rows):
        a, b = lax.rem(self.m + k + 4, 4), lax.rem(self.o + j + 4, 4)
        return self.full.at[(a, b, self.half, *rows)]

    def send(self, ref, device):
        return self.link.send(ref, ref, device)

    def across(self, k):
        piece = self.at(k, 0)
        self.p.append(self.send(piece, self.second(1)))
        self.q.append(self.send(piece, self.second(-1)))

    def start(self):
        piece = self.at(0, 0)
        self.a_p = self.send(piece, self.first(1))
        self.a_m = self.send(piece, self.first(-1))
        self.across(0)

    def near(self):
        self.a_p.wait_recv()
        self.b_p = self.send(self.at(-1, 0, slice(0, 32)), self.first(1))
        self.a_m.wait_recv()
        self.b_m = self.send(self.at(1, 0, slice(32, 64)), self.first(-1))

    def far(self):
        self.b_p.wait_recv()
        self.b_m.wait_recv()

    def relay(self, n):
        k = (0, -1, 1, 2)[n]
        self.p[n].wait_recv()
        self.p[n] = self.send(self.at(k, -1, slice(0, 32)), self.second(1))
        self.q[n].wait_recv()
        self.q[n] = self.send(self.at(k, 1, slice(32, 64)), self.second(-1))

    def finish(self):
        for copy in self.p + self.q:
            copy.wait_recv()

    def group(self, j):
        return (slice(None), lax.rem(self.o + j + 4, 4), self.half)


class ScatterZ:
    def __init__(self, link, where, full, side, right, left, out):
        self.link, self.w, self.full, self.side = link, where, full, side
        self.bufs, self.out = {1: right, -1: left}, out
        self.moves = {}

    def swap(self):
        other = 1 - self.w.core
        self.pair = [
            self.link.send(self.full.at[:, other + 2 * j], self.side.at[:, j], self.w.sibling)
            for j in range(2)
        ]

    def both(self, k, half):
        to = lax.rem(self.w.z + k + NZ, NZ)
        a, j = lax.div(to, 2), lax.rem(to, 2)
        at = (a, 2 * j + self.w.core, half)
        return at, self.full[at].astype(F32) + self.side[a, j, half].astype(F32)

    def move(self, way, n, half):
        at, total = self.both(way * (4 - n), half)
        if n >= 2:
            self.moves[way, half].wait_recv()
            total = total + self.bufs[way][n - 1, half].astype(F32)
        if n == 2 and half == self.long(way):
            self.skips[way].wait_recv()
            total = total + self.bufs[way][0, half].astype(F32)
        self.full[at] = total.astype(BF)
        to = self.w.Z(2 * way if n == 0 else way)
        copy = self.link.send(self.full.at[at], self.bufs[way].at[n, half], to)
        if n == 0:
            self.skips[way] = copy
        else:
            self.moves[way, half] = copy

    def long(self, way):
        return 0 if way == 1 else 1

    def begin(self):
        self.skips = {}
        for copy in self.pair:
            copy.wait_recv()
        for way in (1, -1):
            self.move(way, 0, self.long(way))
        for half in range(2):
            for way in (1, -1):
                self.move(way, 1, half if way == 1 else 1 - half)

    def step(self, n):
        for turn in range(2):
            for way in (1, -1):
                self.move(way, n, 1 - self.long(way) if turn == 0 else self.long(way))

    def finish(self):
        for half in range(2):
            total = self.both(0, half)[1]
            for way in (1, -1) if half == 1 else (-1, 1):
                self.moves[way, half].wait_recv()
                total = total + self.bufs[way][3, half].astype(F32)
            self.out[half] = total.astype(BF)


class Where:
    def __init__(self):
        r, c = lax.axis_index("row"), lax.axis_index("col")
        self.r, self.c = r, c
        self.x, self.y = lax.div(r, NY), lax.rem(r, NY)
        self.z, self.core = lax.div(c, 2), lax.rem(c, 2)
        self.sibling = (r, 2 * self.z + 1 - self.core)
        near, toward = lax.div(self.z, 2), 1 - 2 * lax.rem(self.z, 2)
        self.groups = [lax.rem(near + k + 4, 4) for k in (0, -toward, toward, 2)]

    def order(self, half):
        return (self.x, self.y, self.X, self.Y) if half == 0 else (self.y, self.x, self.Y, self.X)

    def X(self, k):
        return (lax.rem(self.x + k + NX, NX) * NY + self.y, self.c)

    def Y(self, k):
        return (self.x * NY + lax.rem(self.y + k + NY, NY), self.c)

    def Z(self, k):
        return (self.r, lax.rem(self.z + k + NZ, NZ) * 2 + self.core)


def kernel(
    tok, go, wg, wu, wd, gm, um, dm,
    lo, ig, gg, ug, dg,
    t_all, g_all, tt, gt, w, wdm, p_gu, p_hg,
    ra1, ra2, sa, qa1, qa2, rb1, rb2, sb, qb1, qb2,
    ha1, ha2, hsa, hqa1, hqa2, hb1, hb2, hsb, hqb1, hqb2,
    hid, gr, silu_s, slope_s, lop, igp, lo_side, ig_side, lo_r, lo_l, ig_r, ig_l,
    send_sem, recv_sem, load_sem,
):
    where = Where()
    link = Link(send_sem, recv_sem)

    loads = [
        pltpu.make_async_copy(wg, w.at[:, 0:F], load_sem.at[0]),
        pltpu.make_async_copy(wu, w.at[:, F : 2 * F], load_sem.at[1]),
        pltpu.make_async_copy(wd, wdm, load_sem.at[2]),
    ]
    for load in loads:
        load.start()

    barrier = pltpu.get_barrier_semaphore()
    near = (where.X(1), where.X(-1), where.Y(1), where.Y(-1), where.Z(1), where.Z(-1), where.Z(2), where.Z(-2), where.sibling)
    for device in near:
        pl.semaphore_signal(barrier, inc=1, device_id=device, device_id_type=MESH)
    pl.semaphore_wait(barrier, len(near))

    tz = GatherZ(link, where, t_all, tok)
    gz = GatherZ(link, where, g_all, go)
    tz.start()

    for load in loads:
        load.wait()

    @pl.loop(0, 4)
    def _(i):
        rows = pl.ds(pl.multiple_of(i * BLK, BLK), BLK)
        for m_ref, base in ((gm, 0), (um, F)):
            for j in range(7):
                cols = pl.ds(base + j * BLK, BLK)
                w[rows, cols] = (w[rows, cols].astype(F32) * m_ref[i, j].astype(F32)).astype(BF)

    gu = [
        ScatterXY(link, where, 0, p_gu, (ra1, ra2, sa, qa1, qa2)),
        ScatterXY(link, where, 1, p_gu, (rb1, rb2, sb, qb1, qb2)),
    ]
    hg = [
        ScatterXY(link, where, 0, p_hg, (ha1, ha2, hsa, hqa1, hqa2)),
        ScatterXY(link, where, 1, p_hg, (hb1, hb2, hsb, hqb1, hqb2)),
    ]

    def part_gu(n):
        g = where.groups[n]

        @pl.loop(0, 2)
        def _(n):
            cols = pl.ds(pl.multiple_of(n * F, BLK), F)
            part = dot_nn(t_all[g].reshape(512, D), w[:, cols])
            p_gu[g, :, :, :, cols] = part.astype(BF).reshape(4, 2, 64, F)

        for s in gu:
            s.launch(g)

    def part_hg(n):
        g = where.groups[n]
        p_hg[g] = dot_nt(g_all[g].reshape(512, D), wdm[...]).astype(BF).reshape(4, 2, 64, F)
        for s in hg:
            s.launch(g)

    def sums(scatter, n):
        for s in scatter:
            s.sums(where.groups[n])

    def transpose(src, dst, first, last):
        @pl.loop(first, last)
        def _(c):
            block = src[lax.div(c, 4), lax.rem(c, 4)].reshape(BLK, D)
            dst[:, pl.ds(pl.multiple_of(c * BLK, BLK), BLK)] = block.T

    tz.step(1)
    tz.ready(0, 3)
    part_gu(0)
    tz.step(2)
    tz.ready(3, 5)
    part_gu(1)
    tz.step(3)
    gz.start()
    tz.ready(5, 7)
    part_gu(2)
    tz.last()
    tz.ready(7, 8)
    part_gu(3)

    @pl.loop(0, 7)
    def _(i):
        rows = pl.ds(pl.multiple_of(i * BLK, BLK), BLK)
        for j in range(4):
            cols = pl.ds(j * BLK, BLK)
            wdm[rows, cols] = (wdm[rows, cols].astype(F32) * dm[j, i].astype(F32)).astype(BF)

    gz.step(1)
    sums(gu, 0)
    gz.step(2)
    gz.ready(0, 3)
    part_hg(0)
    sums(gu, 1)
    gz.step(3)
    gz.ready(3, 5)
    part_hg(1)
    sums(gu, 2)
    gz.last()
    gz.ready(5, 8)
    part_hg(2)
    part_hg(3)
    sums(gu, 3)
    transpose(t_all, tt, 0, 16)
    for n in range(4):
        sums(hg, n)
    for s in gu:
        s.middle()
    transpose(g_all, gt, 0, 16)
    for s in gu:
        s.sums2()
    for s in hg:
        s.middle()

    hid_ag = [GatherXY(link, where, h, hid) for h in range(2)]
    gr_ag = [GatherXY(link, where, h, gr) for h in range(2)]
    for h in range(2):
        gu[h].arrive()
        gate = gu[h].result(slice(0, F)).astype(BF).astype(F32)
        up = gu[h].result(slice(F, 2 * F)).astype(BF).astype(F32)
        sig = 1.0 / (1.0 + jnp.exp(-gate))
        silu = gate * sig
        silu_s[h] = silu
        slope_s[h] = up * (sig * (1.0 + gate * (1.0 - sig)))
        hid[hid_ag[h].m, hid_ag[h].o, h] = (silu * up).astype(BF)
        hid_ag[h].start()
    lz = ScatterZ(link, where, lop, lo_side, lo_r, lo_l, lo)
    iz = ScatterZ(link, where, igp, ig_side, ig_r, ig_l, ig)

    def out_part(a, first, last):
        @pl.loop(first, last)
        def _(j):
            at = (slice(None), j, a.half)
            lop[at] = dot_nn(rows_of(hid, *at), wdm[...]).astype(BF).reshape(4, 64, D)

    def in_part(a, j):
        at = a.group(j)
        igp[at] = dot_nt(rows_of(gr, *at), w[...]).astype(BF).reshape(4, 64, D)

    def down_part(first, last):
        @pl.loop(first, last)
        def _(j):
            at = pl.ds(pl.multiple_of(j * BLK, BLK), BLK)

            @pl.loop(0, 7)
            def _(i):
                rows = pl.ds(pl.multiple_of(i * BLK, BLK), BLK)
                right = hid[:, :, :, :, rows].reshape(2048, BLK)
                part = dot_nn(gt[at, :], right) * dm[j, i].astype(F32)
                dg[rows, at] = part.T.astype(BF)

    for s in hg:
        s.sums2()
    for a in hid_ag:
        a.near()
    for a in hid_ag:
        a.across(-1)
        a.across(1)
    for h in range(2):
        hg[h].arrive()
        hgrad = hg[h].result(slice(0, F))
        gr[gr_ag[h].m, gr_ag[h].o, h, :, 0:F] = (hgrad * slope_s[h]).astype(BF)
        gr[gr_ag[h].m, gr_ag[h].o, h, :, F : 2 * F] = (hgrad * silu_s[h]).astype(BF)
        gr_ag[h].start()
    for a in hid_ag:
        a.far()
        a.across(2)
    for n in range(3):
        for a in hid_ag:
            a.relay(n)
    for a in gr_ag:
        a.near()
    for a in hid_ag:
        a.relay(3)
    for a in gr_ag:
        a.across(-1)
        a.across(1)
    for a in gr_ag:
        a.far()
        a.across(2)
    for a in hid_ag:
        a.finish()
    for a in hid_ag:
        out_part(a, 0, 4)
    lz.swap()
    for a in gr_ag:
        a.relay(0)
    lz.begin()
    for a in gr_ag:
        in_part(a, 0)
    for a in gr_ag:
        a.relay(1)
    down_part(0, 1)
    for a in gr_ag:
        a.relay(2)
    lz.step(2)
    down_part(1, 2)
    for a in gr_ag:
        a.relay(3)
    lz.step(3)
    down_part(2, 4)
    lz.finish()
    for a in gr_ag:
        in_part(a, -1)
        in_part(a, 1)
    for a in gr_ag:
        a.finish()
        in_part(a, 2)
    iz.swap()

    def weight_part(m_ref, out, base, first, last):
        @pl.loop(first, last)
        def _(j):
            cols = pl.ds(pl.multiple_of(base + j * BLK, BLK), BLK)
            right = gr[:, :, :, :, cols].reshape(2048, BLK)
            part = dot_nn(tt[...], right)
            at = pl.ds(pl.multiple_of(j * BLK, BLK), BLK)
            for i in range(4):
                rows = slice(i * BLK, (i + 1) * BLK)
                out[rows, at] = (part[rows] * m_ref[i, j].astype(F32)).astype(BF)

    iz.begin()
    weight_part(gm, gg, 0, 0, 5)
    iz.step(2)
    weight_part(gm, gg, 0, 5, 7)
    weight_part(um, ug, F, 0, 3)
    iz.step(3)
    weight_part(um, ug, F, 3, 7)
    iz.finish()
    link.drain()


def scatter_bufs(n):
    return [
        pltpu.VMEM((2, 2, 64, n), BF),
        pltpu.VMEM((2, 4, 64, n), BF),
        pltpu.VMEM((4, 64, n), BF),
        pltpu.VMEM((2, 32, n), BF),
        pltpu.VMEM((2, 64, n), BF),
    ]


def hand_over(*refs):
    ins, outs, bufs, sems = refs[:5], refs[5:10], refs[10:15], refs[15]
    first = [pltpu.make_async_copy(ins[i], bufs[i], sems.at[0, i]) for i in range(5)]
    second = [pltpu.make_async_copy(bufs[i], outs[i], sems.at[1, i]) for i in range(5)]
    for copy in first:
        copy.start()
    for i in range(5):
        first[i].wait()
        second[i].start()
    for copy in second:
        copy.wait()


def body(tokens, grad_out, gate_weight, up_weight, down_weight, gate_mask, up_mask, down_mask):
    vmem = pl.BlockSpec(memory_space=pltpu.VMEM)
    smem = pl.BlockSpec(memory_space=pltpu.SMEM)
    anywhere = pl.BlockSpec(memory_space=pl.ANY)
    chunks = (4, 4, 2, 64)
    lo, ig, gg, ug, dg = pl.pallas_call(
        kernel,
        out_shape=(
            jax.ShapeDtypeStruct((2, 64, D), BF),
            jax.ShapeDtypeStruct((2, 64, D), BF),
            jax.ShapeDtypeStruct((D, F), BF),
            jax.ShapeDtypeStruct((D, F), BF),
            jax.ShapeDtypeStruct((F, D), BF),
        ),
        in_specs=[vmem, vmem, anywhere, anywhere, anywhere, smem, smem, smem],
        out_specs=(vmem,) * 5,
        scratch_shapes=[
            pltpu.VMEM((*chunks, D), BF),
            pltpu.VMEM((*chunks, D), BF),
            pltpu.VMEM((D, 2048), BF),
            pltpu.VMEM((D, 2048), BF),
            pltpu.VMEM((D, 2 * F), BF),
            pltpu.VMEM((F, D), BF),
            pltpu.VMEM((*chunks, 2 * F), BF),
            pltpu.VMEM((*chunks, F), BF),
            *scatter_bufs(2 * F), *scatter_bufs(2 * F),
            *scatter_bufs(F), *scatter_bufs(F),
            pltpu.VMEM((*chunks, F), BF),
            pltpu.VMEM((*chunks, 2 * F), BF),
            pltpu.VMEM((2, 64, F), F32),
            pltpu.VMEM((2, 64, F), F32),
            pltpu.VMEM((*chunks, D), BF),
            pltpu.VMEM((*chunks, D), BF),
            pltpu.VMEM((4, 2, 2, 64, D), BF),
            pltpu.VMEM((4, 2, 2, 64, D), BF),
            *[pltpu.VMEM((4, 2, 64, D), BF)] * 4,
            pltpu.SemaphoreType.DMA((NSEM,)),
            pltpu.SemaphoreType.DMA((NSEM,)),
            pltpu.SemaphoreType.DMA((3,)),
        ],
        compiler_params=pltpu.CompilerParams(
            collective_id=0, has_side_effects=True, vmem_limit_bytes=63 * 2**20
        ),
        cost_estimate=pl.CostEstimate(flops=2 * 9 * 2048 * D * F, bytes_accessed=8 * 2**20, transcendentals=0),
    )(
        tokens.reshape(2, 64, D), grad_out.reshape(2, 64, D), gate_weight, up_weight, down_weight,
        gate_mask, up_mask, down_mask.T,
    )
    hbm = pl.BlockSpec(memory_space=pltpu.HBM)
    results = (lo.reshape(BLK, D), ig.reshape(BLK, D), gg, ug, dg)
    return pl.pallas_call(
        hand_over,
        out_shape=tuple(jax.ShapeDtypeStruct(r.shape, r.dtype) for r in results),
        in_specs=[hbm] * 5,
        out_specs=(hbm,) * 5,
        scratch_shapes=[*[pltpu.VMEM(r.shape, r.dtype) for r in results], pltpu.SemaphoreType.DMA((2, 5))],
        compiler_params=pltpu.CompilerParams(vmem_limit_bytes=63 * 2**20),
    )(*results)


def solution(mesh):
    wide, tall = P("row", "col"), P("col", "row")
    return jax.shard_map(
        body,
        mesh=mesh,
        in_specs=(tall, tall, wide, wide, tall, wide, wide, tall),
        out_specs=(tall, tall, wide, wide, tall),
        check_vma=False,
    )
```

```python
import jax
import jax.numpy as jnp
from jax import lax
from jax.experimental import pallas as pl
from jax.experimental.pallas import tpu as pltpu
from jax.sharding import PartitionSpec as P

BLK = 128
NX, NY, NZ = 4, 4, 8
F = 896
D = 512
F32, BF = jnp.float32, jnp.bfloat16
MESH = pl.DeviceIdType.MESH
NSEM = 240


def rows_of(ref, *lead):
    value = ref[lead]
    return value.reshape(256, value.shape[-1])


def dot_nn(a, b):
    return jnp.dot(a, b, preferred_element_type=F32)


def dot_nt(a, b):
    return lax.dot_general(a, b, (((1,), (1,)), ((), ())), preferred_element_type=F32)


class Link:
    def __init__(self, send_sem, recv_sem):
        self.send_sem, self.recv_sem, self.copies = send_sem, recv_sem, []

    def prepare(self, src, dst, device):
        at = len(self.copies)
        copy = pltpu.make_async_remote_copy(
            src_ref=src, dst_ref=dst, send_sem=self.send_sem.at[at], recv_sem=self.recv_sem.at[at],
            device_id=device, device_id_type=MESH,
        )
        self.copies.append(copy)
        return copy

    def send(self, src, dst, device):
        copy = self.prepare(src, dst, device)
        copy.start()
        return copy

    def drain(self):
        for copy in self.copies:
            copy.wait_send()


class GatherZ:
    def __init__(self, link, where, full, own):
        self.link, self.w, self.full, self.own = link, where, full, own
        self.moves = {}

    def slot(self, k, *half):
        chunk = lax.rem(self.w.z + k + NZ, NZ) * 2 + self.w.core
        return self.full.at[(lax.div(chunk, 4), lax.rem(chunk, 4), *half)]

    def move(self, way, k, half):
        ref = self.slot(k, half)
        self.moves[way, half] = self.link.send(ref, ref, self.w.Z(way))

    def start(self):
        own = self.slot(0)
        own[...] = self.own[...]
        for half in range(2):
            for way in (1, -1):
                self.move(way, 0, half if way == 1 else 1 - half)
        self.side = [self.link.send(own, own, self.w.sibling)]

    def step(self, k):
        for turn in range(2):
            for way in (1, -1):
                half = turn if way == 1 else 1 - turn
                self.moves[way, half].wait_recv()
                if k < 3 or turn == 0:
                    self.move(way, -way * k, half)
        for way in (1, -1):
            got = self.slot(-way * k)
            self.side.append(self.link.send(got, got, self.w.sibling))

    def last(self):
        self.moves[1, 0].wait_recv()
        self.moves[-1, 1].wait_recv()
        got = self.slot(4)
        self.side.append(self.link.send(got, got, self.w.sibling))

    def ready(self, first, last):
        for copy in self.side[first:last]:
            copy.wait_recv()


class ScatterXY:
    def __init__(self, link, where, half, full, bufs):
        self.link, self.half, self.full = link, half, full
        self.r1, self.r2, self.s, self.q1, self.q2 = bufs
        self.m, self.o, self.first, self.second = where.order(half)
        lo, hi = slice(0, 2), slice(2, 4)
        prepare = self.link.prepare
        self.far = [
            prepare(self.part(2, lo), self.r1.at[0], self.first(1)),
            prepare(self.part(2, hi), self.r1.at[1], self.first(-1)),
        ]
        self.plain = [
            prepare(self.part(1, hi), self.r2.at[0, hi], self.first(1)),
            prepare(self.part(-1, lo), self.r2.at[1, lo], self.first(-1)),
        ]
        self.summed = [
            prepare(self.part(1, lo), self.r2.at[0, lo], self.first(1)),
            prepare(self.part(-1, hi), self.r2.at[1, hi], self.first(-1)),
        ]

    def index(self, k, o):
        return (lax.rem(self.m + k + 4, 4), o, self.half)

    def part(self, k, o):
        return self.full.at[self.index(k, o)]

    def launch(self, group):
        away = lax.rem(group - self.m + 4, 4)

        @pl.when(away == 2)
        def _():
            for copy in self.far:
                copy.start()

        for i, k in ((0, 1), (1, 3)):

            @pl.when(away == k)
            def _():
                self.plain[i].start()

    def sums(self, group):
        away = lax.rem(group - self.m + 4, 4)
        for i, k, o in ((0, 1, 0), (1, 3, 2)):

            @pl.when(away == k)
            def _():
                self.far[i].wait_recv()
                for j in range(2):
                    at = self.index(k, o + j)
                    self.full[at] = (self.full[at].astype(F32) + self.r1[i, j].astype(F32)).astype(BF)
                self.summed[i].start()

    def middle(self):
        for copy in self.plain + self.summed:
            copy.wait_recv()
        for k in (2, 1, 3, 0):
            i = lax.rem(self.o + k, 4)
            at = self.index(0, i)
            self.s[i] = (
                self.full[at].astype(F32) + self.r2[0, i].astype(F32) + self.r2[1, i].astype(F32)
            ).astype(BF)
        p, q, m = (lax.rem(self.o + k, 4) for k in (1, 2, 3))
        self.d_p = self.link.send(self.s.at[q, 0:32], self.q1.at[0], self.second(1))
        self.d_m = self.link.send(self.s.at[q, 32:64], self.q1.at[1], self.second(-1))
        self.e_p = self.link.send(self.s.at[p, 32:64], self.q2.at[0, 32:64], self.second(1))
        self.e_m = self.link.send(self.s.at[m, 0:32], self.q2.at[1, 0:32], self.second(-1))

    def sums2(self):
        p, m = (lax.rem(self.o + k, 4) for k in (1, 3))
        self.d_p.wait_recv()
        self.s[p, 0:32] = (self.s[p, 0:32].astype(F32) + self.q1[0].astype(F32)).astype(BF)
        self.f_p = self.link.send(self.s.at[p, 0:32], self.q2.at[0, 0:32], self.second(1))
        self.d_m.wait_recv()
        self.s[m, 32:64] = (self.s[m, 32:64].astype(F32) + self.q1[1].astype(F32)).astype(BF)
        self.f_m = self.link.send(self.s.at[m, 32:64], self.q2.at[1, 32:64], self.second(-1))

    def arrive(self):
        for copy in (self.e_p, self.e_m, self.f_p, self.f_m):
            copy.wait_recv()

    def result(self, cols):
        return (
            self.s[self.o, :, cols].astype(F32)
            + self.q2[0, :, cols].astype(F32)
            + self.q2[1, :, cols].astype(F32)
        )


class GatherXY:
    def __init__(self, link, where, half, full):
        self.link, self.half, self.full = link, half, full
        self.m, self.o, self.first, self.second = where.order(half)
        self.p, self.q = [], []

    def at(self, k, j, *rows):
        a, b = lax.rem(self.m + k + 4, 4), lax.rem(self.o + j + 4, 4)
        return self.full.at[(a, b, self.half, *rows)]

    def send(self, ref, device):
        return self.link.send(ref, ref, device)

    def across(self, k):
        piece = self.at(k, 0)
        self.p.append(self.send(piece, self.second(1)))
        self.q.append(self.send(piece, self.second(-1)))

    def start(self):
        piece = self.at(0, 0)
        self.a_p = self.send(piece, self.first(1))
        self.a_m = self.send(piece, self.first(-1))
        self.across(0)

    def near(self):
        self.a_p.wait_recv()
        self.b_p = self.send(self.at(-1, 0, slice(0, 32)), self.first(1))
        self.a_m.wait_recv()
        self.b_m = self.send(self.at(1, 0, slice(32, 64)), self.first(-1))

    def far(self):
        self.b_p.wait_recv()
        self.b_m.wait_recv()

    def relay(self, n):
        k = (0, -1, 1, 2)[n]
        self.p[n].wait_recv()
        self.p[n] = self.send(self.at(k, -1, slice(0, 32)), self.second(1))
        self.q[n].wait_recv()
        self.q[n] = self.send(self.at(k, 1, slice(32, 64)), self.second(-1))

    def finish(self):
        for copy in self.p + self.q:
            copy.wait_recv()

    def group(self, j):
        return (slice(None), lax.rem(self.o + j + 4, 4), self.half)


class ScatterZ:
    def __init__(self, link, where, full, side, right, left, out):
        self.link, self.w, self.full, self.side = link, where, full, side
        self.bufs, self.out = {1: right, -1: left}, out
        self.moves = {}

    def swap(self):
        other = 1 - self.w.core
        self.pair = [
            self.link.send(self.full.at[:, other + 2 * j], self.side.at[:, j], self.w.sibling)
            for j in range(2)
        ]

    def both(self, k, half):
        to = lax.rem(self.w.z + k + NZ, NZ)
        a, j = lax.div(to, 2), lax.rem(to, 2)
        at = (a, 2 * j + self.w.core, half)
        return at, self.full[at].astype(F32) + self.side[a, j, half].astype(F32)

    def move(self, way, n, half):
        at, total = self.both(way * (4 - n), half)
        if n >= 2:
            self.moves[way, half].wait_recv()
            total = total + self.bufs[way][n - 1, half].astype(F32)
        if n == 2 and half == self.long(way):
            self.skips[way].wait_recv()
            total = total + self.bufs[way][0, half].astype(F32)
        self.full[at] = total.astype(BF)
        to = self.w.Z(2 * way if n == 0 else way)
        copy = self.link.send(self.full.at[at], self.bufs[way].at[n, half], to)
        if n == 0:
            self.skips[way] = copy
        else:
            self.moves[way, half] = copy

    def long(self, way):
        return 0 if way == 1 else 1

    def begin(self):
        self.skips = {}
        for copy in self.pair:
            copy.wait_recv()
        for way in (1, -1):
            self.move(way, 0, self.long(way))
        for half in range(2):
            for way in (1, -1):
                self.move(way, 1, half if way == 1 else 1 - half)

    def step(self, n):
        for turn in range(2):
            for way in (1, -1):
                self.move(way, n, 1 - self.long(way) if turn == 0 else self.long(way))

    def finish(self):
        for half in range(2):
            total = self.both(0, half)[1]
            for way in (1, -1) if half == 1 else (-1, 1):
                self.moves[way, half].wait_recv()
                total = total + self.bufs[way][3, half].astype(F32)
            self.out[half] = total.astype(BF)


class Where:
    def __init__(self):
        r, c = lax.axis_index("row"), lax.axis_index("col")
        self.r, self.c = r, c
        self.x, self.y = lax.div(r, NY), lax.rem(r, NY)
        self.z, self.core = lax.div(c, 2), lax.rem(c, 2)
        self.sibling = (r, 2 * self.z + 1 - self.core)
        near, toward = lax.div(self.z, 2), 1 - 2 * lax.rem(self.z, 2)
        self.groups = [lax.rem(near + k + 4, 4) for k in (0, -toward, toward, 2)]

    def order(self, half):
        return (self.x, self.y, self.X, self.Y) if half == 0 else (self.y, self.x, self.Y, self.X)

    def X(self, k):
        return (lax.rem(self.x + k + NX, NX) * NY + self.y, self.c)

    def Y(self, k):
        return (self.x * NY + lax.rem(self.y + k + NY, NY), self.c)

    def Z(self, k):
        return (self.r, lax.rem(self.z + k + NZ, NZ) * 2 + self.core)


def kernel(
    tok, go, wg, wu, wd, gm, um, dm,
    lo, ig, gg, ug, dg,
    t_all, g_all, tt, gt, w, wdm, p_gu, p_hg,
    ra1, ra2, sa, qa1, qa2, rb1, rb2, sb, qb1, qb2,
    ha1, ha2, hsa, hqa1, hqa2, hb1, hb2, hsb, hqb1, hqb2,
    hid, gr, silu_s, slope_s, lop, igp, lo_side, ig_side, lo_r, lo_l, ig_r, ig_l,
    send_sem, recv_sem, load_sem,
):
    where = Where()
    link = Link(send_sem, recv_sem)

    loads = [
        pltpu.make_async_copy(wg, w.at[:, 0:F], load_sem.at[0]),
        pltpu.make_async_copy(wu, w.at[:, F : 2 * F], load_sem.at[1]),
        pltpu.make_async_copy(wd, wdm, load_sem.at[2]),
    ]
    for load in loads:
        load.start()

    barrier = pltpu.get_barrier_semaphore()
    near = (where.X(1), where.X(-1), where.Y(1), where.Y(-1), where.Z(1), where.Z(-1), where.Z(2), where.Z(-2), where.sibling)
    for device in near:
        pl.semaphore_signal(barrier, inc=1, device_id=device, device_id_type=MESH)
    pl.semaphore_wait(barrier, len(near))

    tz = GatherZ(link, where, t_all, tok)
    gz = GatherZ(link, where, g_all, go)
    tz.start()

    for load in loads:
        load.wait()

    @pl.loop(0, 4)
    def _(i):
        rows = pl.ds(pl.multiple_of(i * BLK, BLK), BLK)
        for m_ref, base in ((gm, 0), (um, F)):
            for j in range(7):
                cols = pl.ds(base + j * BLK, BLK)
                w[rows, cols] = (w[rows, cols].astype(F32) * m_ref[i, j].astype(F32)).astype(BF)

    gu = [
        ScatterXY(link, where, 0, p_gu, (ra1, ra2, sa, qa1, qa2)),
        ScatterXY(link, where, 1, p_gu, (rb1, rb2, sb, qb1, qb2)),
    ]
    hg = [
        ScatterXY(link, where, 0, p_hg, (ha1, ha2, hsa, hqa1, hqa2)),
        ScatterXY(link, where, 1, p_hg, (hb1, hb2, hsb, hqb1, hqb2)),
    ]

    def part_gu(n):
        g = where.groups[n]

        @pl.loop(0, 2)
        def _(n):
            cols = pl.ds(pl.multiple_of(n * F, BLK), F)
            part = dot_nn(t_all[g].reshape(512, D), w[:, cols])
            p_gu[g, :, :, :, cols] = part.astype(BF).reshape(4, 2, 64, F)

        for s in gu:
            s.launch(g)

    def part_hg(n):
        g = where.groups[n]
        p_hg[g] = dot_nt(g_all[g].reshape(512, D), wdm[...]).astype(BF).reshape(4, 2, 64, F)
        for s in hg:
            s.launch(g)

    def sums(scatter, n):
        for s in scatter:
            s.sums(where.groups[n])

    def transpose(src, dst, first, last):
        @pl.loop(first, last)
        def _(c):
            block = src[lax.div(c, 4), lax.rem(c, 4)].reshape(BLK, D)
            dst[:, pl.ds(pl.multiple_of(c * BLK, BLK), BLK)] = block.T

    tz.step(1)
    tz.ready(0, 3)
    part_gu(0)
    tz.step(2)
    tz.ready(3, 5)
    part_gu(1)
    tz.step(3)
    gz.start()
    tz.ready(5, 7)
    part_gu(2)
    tz.last()
    tz.ready(7, 8)
    part_gu(3)

    @pl.loop(0, 7)
    def _(i):
        rows = pl.ds(pl.multiple_of(i * BLK, BLK), BLK)
        for j in range(4):
            cols = pl.ds(j * BLK, BLK)
            wdm[rows, cols] = (wdm[rows, cols].astype(F32) * dm[j, i].astype(F32)).astype(BF)

    gz.step(1)
    sums(gu, 0)
    sums(gu, 1)
    gz.step(2)
    gz.ready(0, 3)
    part_hg(0)
    sums(gu, 2)
    gz.step(3)
    gz.ready(3, 5)
    part_hg(1)
    gz.ready(5, 7)
    part_hg(2)
    sums(gu, 3)
    gz.last()
    gz.ready(7, 8)
    part_hg(3)
    for n in range(4):
        sums(hg, n)
    for s in gu:
        s.middle()
    transpose(t_all, tt, 0, 16)
    transpose(g_all, gt, 0, 16)
    for s in gu:
        s.sums2()
    for s in hg:
        s.middle()

    hid_ag = [GatherXY(link, where, h, hid) for h in range(2)]
    gr_ag = [GatherXY(link, where, h, gr) for h in range(2)]
    for h in range(2):
        gu[h].arrive()
        gate = gu[h].result(slice(0, F)).astype(BF).astype(F32)
        up = gu[h].result(slice(F, 2 * F)).astype(BF).astype(F32)
        sig = 1.0 / (1.0 + jnp.exp(-gate))
        silu = gate * sig
        silu_s[h] = silu
        slope_s[h] = up * (sig * (1.0 + gate * (1.0 - sig)))
        hid[hid_ag[h].m, hid_ag[h].o, h] = (silu * up).astype(BF)
        hid_ag[h].start()
    lz = ScatterZ(link, where, lop, lo_side, lo_r, lo_l, lo)
    iz = ScatterZ(link, where, igp, ig_side, ig_r, ig_l, ig)

    def out_part():
        @pl.loop(0, 4)
        def _(d):
            lop[d] = dot_nn(hid[d].reshape(512, F), wdm[...]).astype(BF).reshape(4, 2, 64, D)

    def in_part(a, j):
        at = a.group(j)
        igp[at] = dot_nt(rows_of(gr, *at), w[...]).astype(BF).reshape(4, 64, D)

    def down_tile(first, width):
        right = hid[:, :, :, :, pl.ds(first, width)].reshape(2048, width)
        part = dot_nn(gt[...], right)
        for i in range(width // BLK):
            for j in range(4):
                block = part[j * BLK : (j + 1) * BLK, i * BLK : (i + 1) * BLK] * dm[j, first // BLK + i].astype(F32)
                dg[pl.ds(first + i * BLK, BLK), j * BLK : (j + 1) * BLK] = block.T.astype(BF)

    def down_part(first, last):
        @pl.loop(first, min(last, 3))
        def _(n):
            down_tile(pl.multiple_of(n * 256, 256), 256)

        if last == 4:
            down_tile(768, BLK)

    for s in hg:
        s.sums2()
    for a in hid_ag:
        a.near()
    for a in hid_ag:
        a.across(-1)
        a.across(1)
    for h in range(2):
        hg[h].arrive()
        hgrad = hg[h].result(slice(0, F))
        gr[gr_ag[h].m, gr_ag[h].o, h, :, 0:F] = (hgrad * slope_s[h]).astype(BF)
        gr[gr_ag[h].m, gr_ag[h].o, h, :, F : 2 * F] = (hgrad * silu_s[h]).astype(BF)
        gr_ag[h].start()
    for a in hid_ag:
        a.far()
        a.across(2)
    for n in range(3):
        for a in hid_ag:
            a.relay(n)
    for a in gr_ag:
        a.near()
    for a in hid_ag:
        a.relay(3)
    for a in gr_ag:
        a.across(-1)
        a.across(1)
    for a in gr_ag:
        a.relay(0)
    for a in gr_ag:
        a.far()
        a.across(2)
    for a in hid_ag:
        a.finish()
    for a in gr_ag:
        a.relay(1)
    out_part()
    lz.swap()
    down_part(0, 1)
    for a in gr_ag:
        a.relay(2)
    lz.begin()
    for a in gr_ag:
        in_part(a, 0)
    down_part(1, 2)
    for a in gr_ag:
        a.relay(3)
    for a in gr_ag:
        in_part(a, -1)
        in_part(a, 1)
    lz.step(2)
    down_part(2, 4)
    for a in gr_ag:
        a.finish()
        in_part(a, 2)
    iz.swap()
    lz.step(3)

    def weight_tile(m_ref, out, base, first, width):
        right = gr[:, :, :, :, pl.ds(base + first, width)].reshape(2048, width)
        part = dot_nn(tt[...], right)
        for j in range(width // BLK):
            at = pl.ds(first + j * BLK, BLK)
            for i in range(4):
                rows = slice(i * BLK, (i + 1) * BLK)
                live = m_ref[i, first // BLK + j].astype(F32)
                out[rows, at] = (part[rows, j * BLK : (j + 1) * BLK] * live).astype(BF)

    def weight_part(m_ref, out, base, first, last):
        @pl.loop(min(first, 3), min(last, 3))
        def _(n):
            weight_tile(m_ref, out, base, pl.multiple_of(n * 256, 256), 256)

        if last == 4:
            weight_tile(m_ref, out, base, 768, BLK)

    iz.begin()
    weight_part(gm, gg, 0, 0, 3)
    lz.finish()
    iz.step(2)
    weight_part(gm, gg, 0, 3, 4)
    weight_part(um, ug, F, 0, 2)
    iz.step(3)
    weight_part(um, ug, F, 2, 4)
    iz.finish()
    link.drain()


def scatter_bufs(n):
    return [
        pltpu.VMEM((2, 2, 64, n), BF),
        pltpu.VMEM((2, 4, 64, n), BF),
        pltpu.VMEM((4, 64, n), BF),
        pltpu.VMEM((2, 32, n), BF),
        pltpu.VMEM((2, 64, n), BF),
    ]


def hand_over(*refs):
    ins, outs, bufs, sems = refs[:5], refs[5:10], refs[10:15], refs[15]
    first = [pltpu.make_async_copy(ins[i], bufs[i], sems.at[0, i]) for i in range(5)]
    second = [pltpu.make_async_copy(bufs[i], outs[i], sems.at[1, i]) for i in range(5)]
    for copy in first:
        copy.start()
    for i in range(5):
        first[i].wait()
        second[i].start()
    for copy in second:
        copy.wait()


def body(tokens, grad_out, gate_weight, up_weight, down_weight, gate_mask, up_mask, down_mask):
    vmem = pl.BlockSpec(memory_space=pltpu.VMEM)
    smem = pl.BlockSpec(memory_space=pltpu.SMEM)
    anywhere = pl.BlockSpec(memory_space=pl.ANY)
    chunks = (4, 4, 2, 64)
    lo, ig, gg, ug, dg = pl.pallas_call(
        kernel,
        out_shape=(
            jax.ShapeDtypeStruct((2, 64, D), BF),
            jax.ShapeDtypeStruct((2, 64, D), BF),
            jax.ShapeDtypeStruct((D, F), BF),
            jax.ShapeDtypeStruct((D, F), BF),
            jax.ShapeDtypeStruct((F, D), BF),
        ),
        in_specs=[vmem, vmem, anywhere, anywhere, anywhere, smem, smem, smem],
        out_specs=(vmem,) * 5,
        scratch_shapes=[
            pltpu.VMEM((*chunks, D), BF),
            pltpu.VMEM((*chunks, D), BF),
            pltpu.VMEM((D, 2048), BF),
            pltpu.VMEM((D, 2048), BF),
            pltpu.VMEM((D, 2 * F), BF),
            pltpu.VMEM((F, D), BF),
            pltpu.VMEM((*chunks, 2 * F), BF),
            pltpu.VMEM((*chunks, F), BF),
            *scatter_bufs(2 * F), *scatter_bufs(2 * F),
            *scatter_bufs(F), *scatter_bufs(F),
            pltpu.VMEM((*chunks, F), BF),
            pltpu.VMEM((*chunks, 2 * F), BF),
            pltpu.VMEM((2, 64, F), F32),
            pltpu.VMEM((2, 64, F), F32),
            pltpu.VMEM((*chunks, D), BF),
            pltpu.VMEM((*chunks, D), BF),
            pltpu.VMEM((4, 2, 2, 64, D), BF),
            pltpu.VMEM((4, 2, 2, 64, D), BF),
            *[pltpu.VMEM((4, 2, 64, D), BF)] * 4,
            pltpu.SemaphoreType.DMA((NSEM,)),
            pltpu.SemaphoreType.DMA((NSEM,)),
            pltpu.SemaphoreType.DMA((3,)),
        ],
        compiler_params=pltpu.CompilerParams(
            collective_id=0, has_side_effects=True, vmem_limit_bytes=63 * 2**20
        ),
        cost_estimate=pl.CostEstimate(flops=2 * 9 * 2048 * D * F, bytes_accessed=8 * 2**20, transcendentals=0),
    )(
        tokens.reshape(2, 64, D), grad_out.reshape(2, 64, D), gate_weight, up_weight, down_weight,
        gate_mask, up_mask, down_mask.T,
    )
    hbm = pl.BlockSpec(memory_space=pltpu.HBM)
    results = (lo.reshape(BLK, D), ig.reshape(BLK, D), gg, ug, dg)
    return pl.pallas_call(
        hand_over,
        out_shape=tuple(jax.ShapeDtypeStruct(r.shape, r.dtype) for r in results),
        in_specs=[hbm] * 5,
        out_specs=(hbm,) * 5,
        scratch_shapes=[*[pltpu.VMEM(r.shape, r.dtype) for r in results], pltpu.SemaphoreType.DMA((2, 5))],
        compiler_params=pltpu.CompilerParams(vmem_limit_bytes=63 * 2**20),
    )(*results)


def solution(mesh):
    wide, tall = P("row", "col"), P("col", "row")
    return jax.shard_map(
        body,
        mesh=mesh,
        in_specs=(tall, tall, wide, wide, tall, wide, wide, tall),
        out_specs=(tall, tall, wide, wide, tall),
        check_vma=False,
    )
```

```python
import jax
import jax.numpy as jnp
from jax import lax
from jax.experimental import pallas as pl
from jax.experimental.pallas import tpu as pltpu
from jax.sharding import PartitionSpec as P

BLK = 128
NX, NY, NZ = 4, 4, 8
F = 896
D = 512
F32, BF = jnp.float32, jnp.bfloat16
MESH = pl.DeviceIdType.MESH
NSEM = 240


def rows_of(ref, *lead):
    value = ref[lead]
    return value.reshape(256, value.shape[-1])


def dot_nn(a, b):
    return jnp.dot(a, b, preferred_element_type=F32)


def dot_nt(a, b):
    return lax.dot_general(a, b, (((1,), (1,)), ((), ())), preferred_element_type=F32)


class Link:
    def __init__(self, send_sem, recv_sem):
        self.send_sem, self.recv_sem, self.copies = send_sem, recv_sem, []

    def prepare(self, src, dst, device):
        at = len(self.copies)
        copy = pltpu.make_async_remote_copy(
            src_ref=src, dst_ref=dst, send_sem=self.send_sem.at[at], recv_sem=self.recv_sem.at[at],
            device_id=device, device_id_type=MESH,
        )
        self.copies.append(copy)
        return copy

    def send(self, src, dst, device):
        copy = self.prepare(src, dst, device)
        copy.start()
        return copy

    def drain(self):
        for copy in self.copies:
            copy.wait_send()


class GatherZ:
    def __init__(self, link, where, full, own):
        self.link, self.w, self.full, self.own = link, where, full, own
        self.moves = {}

    def slot(self, k, *half):
        chunk = lax.rem(self.w.z + k + NZ, NZ) * 2 + self.w.core
        return self.full.at[(lax.div(chunk, 4), lax.rem(chunk, 4), *half)]

    def move(self, way, k, half):
        ref = self.slot(k, half)
        self.moves[way, half] = self.link.send(ref, ref, self.w.Z(way))

    def start(self):
        own = self.slot(0)
        own[...] = self.own[...]
        for half in range(2):
            for way in (1, -1):
                self.move(way, 0, half if way == 1 else 1 - half)
        self.side = [self.link.send(own, own, self.w.sibling)]

    def step(self, k):
        for turn in range(2):
            for way in (1, -1):
                half = turn if way == 1 else 1 - turn
                self.moves[way, half].wait_recv()
                if k < 3 or turn == 0:
                    self.move(way, -way * k, half)
        for way in (1, -1):
            got = self.slot(-way * k)
            self.side.append(self.link.send(got, got, self.w.sibling))

    def last(self):
        self.moves[1, 0].wait_recv()
        self.moves[-1, 1].wait_recv()
        got = self.slot(4)
        self.side.append(self.link.send(got, got, self.w.sibling))

    def ready(self, first, last):
        for copy in self.side[first:last]:
            copy.wait_recv()


class ScatterXY:
    def __init__(self, link, where, half, full, bufs):
        self.link, self.half, self.full = link, half, full
        self.r1, self.r2, self.s, self.q1, self.q2 = bufs
        self.m, self.o, self.first, self.second = where.order(half)
        lo, hi = slice(0, 2), slice(2, 4)
        prepare = self.link.prepare
        self.far = [
            prepare(self.part(2, lo), self.r1.at[0], self.first(1)),
            prepare(self.part(2, hi), self.r1.at[1], self.first(-1)),
        ]
        self.plain = [
            prepare(self.part(1, hi), self.r2.at[0, hi], self.first(1)),
            prepare(self.part(-1, lo), self.r2.at[1, lo], self.first(-1)),
        ]
        self.summed = [
            prepare(self.part(1, lo), self.r2.at[0, lo], self.first(1)),
            prepare(self.part(-1, hi), self.r2.at[1, hi], self.first(-1)),
        ]

    def index(self, k, o):
        return (lax.rem(self.m + k + 4, 4), o, self.half)

    def part(self, k, o):
        return self.full.at[self.index(k, o)]

    def launch(self, group):
        away = lax.rem(group - self.m + 4, 4)

        @pl.when(away == 2)
        def _():
            for copy in self.far:
                copy.start()

        for i, k in ((0, 1), (1, 3)):

            @pl.when(away == k)
            def _():
                self.plain[i].start()

    def sums(self, group):
        away = lax.rem(group - self.m + 4, 4)
        for i, k, o in ((0, 1, 0), (1, 3, 2)):

            @pl.when(away == k)
            def _():
                self.far[i].wait_recv()
                for j in range(2):
                    at = self.index(k, o + j)
                    self.full[at] = (self.full[at].astype(F32) + self.r1[i, j].astype(F32)).astype(BF)
                self.summed[i].start()

    def middle(self):
        for copy in self.plain + self.summed:
            copy.wait_recv()
        def total(k):
            i = lax.rem(self.o + k, 4)
            at = self.index(0, i)
            self.s[i] = (
                self.full[at].astype(F32) + self.r2[0, i].astype(F32) + self.r2[1, i].astype(F32)
            ).astype(BF)
            return i

        q = total(2)
        self.d_p = self.link.send(self.s.at[q, 0:32], self.q1.at[0], self.second(1))
        self.d_m = self.link.send(self.s.at[q, 32:64], self.q1.at[1], self.second(-1))
        p = total(1)
        self.e_p = self.link.send(self.s.at[p, 32:64], self.q2.at[0, 32:64], self.second(1))
        m = total(3)
        self.e_m = self.link.send(self.s.at[m, 0:32], self.q2.at[1, 0:32], self.second(-1))
        total(0)

    def sums2(self):
        p, m = (lax.rem(self.o + k, 4) for k in (1, 3))
        self.d_p.wait_recv()
        self.s[p, 0:32] = (self.s[p, 0:32].astype(F32) + self.q1[0].astype(F32)).astype(BF)
        self.f_p = self.link.send(self.s.at[p, 0:32], self.q2.at[0, 0:32], self.second(1))
        self.d_m.wait_recv()
        self.s[m, 32:64] = (self.s[m, 32:64].astype(F32) + self.q1[1].astype(F32)).astype(BF)
        self.f_m = self.link.send(self.s.at[m, 32:64], self.q2.at[1, 32:64], self.second(-1))

    def arrive(self):
        for copy in (self.e_p, self.e_m, self.f_p, self.f_m):
            copy.wait_recv()

    def result(self, cols):
        return (
            self.s[self.o, :, cols].astype(F32)
            + self.q2[0, :, cols].astype(F32)
            + self.q2[1, :, cols].astype(F32)
        )


class GatherXY:
    def __init__(self, link, where, half, full):
        self.link, self.half, self.full = link, half, full
        self.m, self.o, self.first, self.second = where.order(half)
        self.p, self.q = [], []

    def at(self, k, j, *rows):
        a, b = lax.rem(self.m + k + 4, 4), lax.rem(self.o + j + 4, 4)
        return self.full.at[(a, b, self.half, *rows)]

    def send(self, ref, device):
        return self.link.send(ref, ref, device)

    def across(self, k):
        piece = self.at(k, 0)
        self.p.append(self.send(piece, self.second(1)))
        self.q.append(self.send(piece, self.second(-1)))

    def start(self):
        piece = self.at(0, 0)
        self.a_p = self.send(piece, self.first(1))
        self.a_m = self.send(piece, self.first(-1))
        self.across(0)

    def near(self):
        self.a_p.wait_recv()
        self.b_p = self.send(self.at(-1, 0, slice(0, 32)), self.first(1))
        self.a_m.wait_recv()
        self.b_m = self.send(self.at(1, 0, slice(32, 64)), self.first(-1))

    def far(self):
        self.b_p.wait_recv()
        self.b_m.wait_recv()

    def relay(self, n):
        k = (0, -1, 1, 2)[n]
        self.p[n].wait_recv()
        self.p[n] = self.send(self.at(k, -1, slice(0, 32)), self.second(1))
        self.q[n].wait_recv()
        self.q[n] = self.send(self.at(k, 1, slice(32, 64)), self.second(-1))

    def finish(self):
        for copy in self.p + self.q:
            copy.wait_recv()

    def group(self, j):
        return (slice(None), lax.rem(self.o + j + 4, 4), self.half)


class ScatterZ:
    def __init__(self, link, where, full, side, right, left, out):
        self.link, self.w, self.full, self.side = link, where, full, side
        self.bufs, self.out = {1: right, -1: left}, out
        self.moves = {}

    def swap(self):
        other = 1 - self.w.core
        self.pair = [
            self.link.send(self.full.at[:, other + 2 * j], self.side.at[:, j], self.w.sibling)
            for j in range(2)
        ]

    def both(self, k, half):
        to = lax.rem(self.w.z + k + NZ, NZ)
        a, j = lax.div(to, 2), lax.rem(to, 2)
        at = (a, 2 * j + self.w.core, half)
        return at, self.full[at].astype(F32) + self.side[a, j, half].astype(F32)

    def move(self, way, n, half):
        at, total = self.both(way * (4 - n), half)
        if n >= 2:
            self.moves[way, half].wait_recv()
            total = total + self.bufs[way][n - 1, half].astype(F32)
        if n == 2 and half == self.long(way):
            self.skips[way].wait_recv()
            total = total + self.bufs[way][0, half].astype(F32)
        self.full[at] = total.astype(BF)
        to = self.w.Z(2 * way if n == 0 else way)
        copy = self.link.send(self.full.at[at], self.bufs[way].at[n, half], to)
        if n == 0:
            self.skips[way] = copy
        else:
            self.moves[way, half] = copy

    def long(self, way):
        return 0 if way == 1 else 1

    def begin(self):
        self.skips = {}
        for copy in self.pair:
            copy.wait_recv()
        for way in (1, -1):
            self.move(way, 0, self.long(way))
        for half in range(2):
            for way in (1, -1):
                self.move(way, 1, half if way == 1 else 1 - half)

    def step(self, n):
        for turn in range(2):
            for way in (1, -1):
                self.move(way, n, 1 - self.long(way) if turn == 0 else self.long(way))

    def finish(self):
        for half in range(2):
            total = self.both(0, half)[1]
            for way in (1, -1) if half == 1 else (-1, 1):
                self.moves[way, half].wait_recv()
                total = total + self.bufs[way][3, half].astype(F32)
            self.out[half] = total.astype(BF)


class Where:
    def __init__(self):
        r, c = lax.axis_index("row"), lax.axis_index("col")
        self.r, self.c = r, c
        self.x, self.y = lax.div(r, NY), lax.rem(r, NY)
        self.z, self.core = lax.div(c, 2), lax.rem(c, 2)
        self.sibling = (r, 2 * self.z + 1 - self.core)
        near, toward = lax.div(self.z, 2), 1 - 2 * lax.rem(self.z, 2)
        self.groups = [lax.rem(near + k + 4, 4) for k in (0, -toward, toward, 2)]

    def order(self, half):
        return (self.x, self.y, self.X, self.Y) if half == 0 else (self.y, self.x, self.Y, self.X)

    def X(self, k):
        return (lax.rem(self.x + k + NX, NX) * NY + self.y, self.c)

    def Y(self, k):
        return (self.x * NY + lax.rem(self.y + k + NY, NY), self.c)

    def Z(self, k):
        return (self.r, lax.rem(self.z + k + NZ, NZ) * 2 + self.core)


def kernel(
    tok, go, wg, wu, wd, gm, um, dm,
    lo, ig, gg_out, ug_out, dg_out,
    gg, ug, dg, t_all, g_all, tt, gt, w, wdm, p_gu, p_hg,
    ra1, ra2, sa, qa1, qa2, rb1, rb2, sb, qb1, qb2,
    ha1, ha2, hsa, hqa1, hqa2, hb1, hb2, hsb, hqb1, hqb2,
    hid, gr, silu_s, slope_s, lop, igp, lo_side, ig_side, lo_r, lo_l, ig_r, ig_l,
    send_sem, recv_sem, load_sem,
):
    where = Where()
    link = Link(send_sem, recv_sem)

    loads = [
        pltpu.make_async_copy(wg, w.at[:, 0:F], load_sem.at[0]),
        pltpu.make_async_copy(wu, w.at[:, F : 2 * F], load_sem.at[1]),
        pltpu.make_async_copy(wd, wdm, load_sem.at[2]),
    ]
    stores = [
        pltpu.make_async_copy(buf, out, load_sem.at[3 + i])
        for i, (buf, out) in enumerate(((dg, dg_out), (gg, gg_out), (ug, ug_out)))
    ]
    for load in loads:
        load.start()

    barrier = pltpu.get_barrier_semaphore()
    near = (where.X(1), where.X(-1), where.Y(1), where.Y(-1), where.Z(1), where.Z(-1), where.Z(2), where.Z(-2), where.sibling)
    for device in near:
        pl.semaphore_signal(barrier, inc=1, device_id=device, device_id_type=MESH)
    pl.semaphore_wait(barrier, len(near))

    tz = GatherZ(link, where, t_all, tok)
    gz = GatherZ(link, where, g_all, go)
    tz.start()

    for load in loads:
        load.wait()

    @pl.loop(0, 4)
    def _(i):
        rows = pl.ds(pl.multiple_of(i * BLK, BLK), BLK)
        for m_ref, base in ((gm, 0), (um, F)):
            for j in range(7):
                cols = pl.ds(base + j * BLK, BLK)
                w[rows, cols] = (w[rows, cols].astype(F32) * m_ref[i, j].astype(F32)).astype(BF)

    gu = [
        ScatterXY(link, where, 0, p_gu, (ra1, ra2, sa, qa1, qa2)),
        ScatterXY(link, where, 1, p_gu, (rb1, rb2, sb, qb1, qb2)),
    ]
    hg = [
        ScatterXY(link, where, 0, p_hg, (ha1, ha2, hsa, hqa1, hqa2)),
        ScatterXY(link, where, 1, p_hg, (hb1, hb2, hsb, hqb1, hqb2)),
    ]

    def part_gu(n):
        g = where.groups[n]

        @pl.loop(0, 2)
        def _(n):
            cols = pl.ds(pl.multiple_of(n * F, BLK), F)
            part = dot_nn(t_all[g].reshape(512, D), w[:, cols])
            p_gu[g, :, :, :, cols] = part.astype(BF).reshape(4, 2, 64, F)

        for s in gu:
            s.launch(g)

    def part_hg(n):
        g = where.groups[n]
        p_hg[g] = dot_nt(g_all[g].reshape(512, D), wdm[...]).astype(BF).reshape(4, 2, 64, F)
        for s in hg:
            s.launch(g)

    def sums(scatter, n):
        for s in scatter:
            s.sums(where.groups[n])

    def transpose(src, dst, first, last):
        @pl.loop(first, last)
        def _(c):
            block = src[lax.div(c, 4), lax.rem(c, 4)].reshape(BLK, D)
            dst[:, pl.ds(pl.multiple_of(c * BLK, BLK), BLK)] = block.T

    tz.step(1)
    tz.ready(0, 3)
    part_gu(0)
    tz.step(2)
    tz.ready(3, 5)
    part_gu(1)
    tz.step(3)
    gz.start()
    tz.ready(5, 7)
    part_gu(2)
    tz.last()
    tz.ready(7, 8)
    part_gu(3)

    @pl.loop(0, 7)
    def _(i):
        rows = pl.ds(pl.multiple_of(i * BLK, BLK), BLK)
        for j in range(4):
            cols = pl.ds(j * BLK, BLK)
            wdm[rows, cols] = (wdm[rows, cols].astype(F32) * dm[j, i].astype(F32)).astype(BF)

    gz.step(1)
    sums(gu, 0)
    sums(gu, 1)
    gz.step(2)
    gz.ready(0, 3)
    part_hg(0)
    sums(gu, 2)
    gz.step(3)
    gz.ready(3, 5)
    part_hg(1)
    gz.ready(5, 7)
    part_hg(2)
    sums(gu, 3)
    gz.last()
    gz.ready(7, 8)
    part_hg(3)
    for n in range(4):
        sums(hg, n)
    for s in gu:
        s.middle()
    transpose(t_all, tt, 0, 16)
    transpose(g_all, gt, 0, 16)
    for s in gu:
        s.sums2()
    for s in hg:
        s.middle()

    hid_ag = [GatherXY(link, where, h, hid) for h in range(2)]
    gr_ag = [GatherXY(link, where, h, gr) for h in range(2)]
    for h in range(2):
        gu[h].arrive()
        gate = gu[h].result(slice(0, F)).astype(BF).astype(F32)
        up = gu[h].result(slice(F, 2 * F)).astype(BF).astype(F32)
        sig = 1.0 / (1.0 + jnp.exp(-gate))
        silu = gate * sig
        silu_s[h] = silu
        slope_s[h] = up * (sig * (1.0 + gate * (1.0 - sig)))
        hid[hid_ag[h].m, hid_ag[h].o, h] = (silu * up).astype(BF)
        hid_ag[h].start()
    lz = ScatterZ(link, where, lop, lo_side, lo_r, lo_l, lo)
    iz = ScatterZ(link, where, igp, ig_side, ig_r, ig_l, ig)

    def out_part():
        @pl.loop(0, 4)
        def _(d):
            lop[d] = dot_nn(hid[d].reshape(512, F), wdm[...]).astype(BF).reshape(4, 2, 64, D)

    def in_part(a, j):
        at = a.group(j)
        igp[at] = dot_nt(rows_of(gr, *at), w[...]).astype(BF).reshape(4, 64, D)

    def down_tile(first, width):
        right = hid[:, :, :, :, pl.ds(first, width)].reshape(2048, width)
        part = dot_nn(gt[...], right)
        for i in range(width // BLK):
            for j in range(4):
                block = part[j * BLK : (j + 1) * BLK, i * BLK : (i + 1) * BLK] * dm[j, first // BLK + i].astype(F32)
                dg[pl.ds(first + i * BLK, BLK), j * BLK : (j + 1) * BLK] = block.T.astype(BF)

    def down_part(first, last):
        @pl.loop(first, min(last, 3))
        def _(n):
            down_tile(pl.multiple_of(n * 256, 256), 256)

        if last == 4:
            down_tile(768, BLK)

    for s in hg:
        s.sums2()
    for a in hid_ag:
        a.near()
    for a in hid_ag:
        a.across(-1)
        a.across(1)
    for h in range(2):
        hg[h].arrive()
        hgrad = hg[h].result(slice(0, F))
        gr[gr_ag[h].m, gr_ag[h].o, h, :, 0:F] = (hgrad * slope_s[h]).astype(BF)
        gr[gr_ag[h].m, gr_ag[h].o, h, :, F : 2 * F] = (hgrad * silu_s[h]).astype(BF)
        gr_ag[h].start()
    for a in hid_ag:
        a.far()
        a.across(2)
    for n in range(3):
        for a in hid_ag:
            a.relay(n)
    for a in gr_ag:
        a.near()
    for a in hid_ag:
        a.relay(3)
    for a in gr_ag:
        a.across(-1)
        a.across(1)
    for a in gr_ag:
        a.relay(0)
    for a in gr_ag:
        a.far()
        a.across(2)
    for a in hid_ag:
        a.finish()
    for a in gr_ag:
        a.relay(1)
    out_part()
    lz.swap()
    down_part(0, 1)
    for a in gr_ag:
        a.relay(2)
    lz.begin()
    for a in gr_ag:
        in_part(a, 0)
    down_part(1, 2)
    for a in gr_ag:
        a.relay(3)
    for a in gr_ag:
        in_part(a, -1)
        in_part(a, 1)
    lz.step(2)
    down_part(2, 4)
    stores[0].start()
    for a in gr_ag:
        a.finish()
        in_part(a, 2)
    iz.swap()
    lz.step(3)

    def weight_tile(m_ref, out, base, first, width):
        right = gr[:, :, :, :, pl.ds(base + first, width)].reshape(2048, width)
        part = dot_nn(tt[...], right)
        for j in range(width // BLK):
            at = pl.ds(first + j * BLK, BLK)
            for i in range(4):
                rows = slice(i * BLK, (i + 1) * BLK)
                live = m_ref[i, first // BLK + j].astype(F32)
                out[rows, at] = (part[rows, j * BLK : (j + 1) * BLK] * live).astype(BF)

    def weight_part(m_ref, out, base, first, last):
        @pl.loop(min(first, 3), min(last, 3))
        def _(n):
            weight_tile(m_ref, out, base, pl.multiple_of(n * 256, 256), 256)

        if last == 4:
            weight_tile(m_ref, out, base, 768, BLK)

    iz.begin()
    weight_part(gm, gg, 0, 0, 3)
    lz.finish()
    iz.step(2)
    weight_part(gm, gg, 0, 3, 4)
    stores[1].start()
    weight_part(um, ug, F, 0, 2)
    iz.step(3)
    weight_part(um, ug, F, 2, 4)
    stores[2].start()
    iz.finish()
    link.drain()
    for store in stores:
        store.wait()


def scatter_bufs(n):
    return [
        pltpu.VMEM((2, 2, 64, n), BF),
        pltpu.VMEM((2, 4, 64, n), BF),
        pltpu.VMEM((4, 64, n), BF),
        pltpu.VMEM((2, 32, n), BF),
        pltpu.VMEM((2, 64, n), BF),
    ]


def hand_over(*refs):
    ins, outs, bufs, sems = refs[:5], refs[5:10], refs[10:15], refs[15]
    first = [pltpu.make_async_copy(ins[i], bufs[i], sems.at[0, i]) for i in range(5)]
    second = [pltpu.make_async_copy(bufs[i], outs[i], sems.at[1, i]) for i in range(5)]
    for copy in first:
        copy.start()
    for i in range(5):
        first[i].wait()
        second[i].start()
    for copy in second:
        copy.wait()


def body(tokens, grad_out, gate_weight, up_weight, down_weight, gate_mask, up_mask, down_mask):
    vmem = pl.BlockSpec(memory_space=pltpu.VMEM)
    smem = pl.BlockSpec(memory_space=pltpu.SMEM)
    anywhere = pl.BlockSpec(memory_space=pl.ANY)
    chunks = (4, 4, 2, 64)
    lo, ig, gg, ug, dg = pl.pallas_call(
        kernel,
        out_shape=(
            jax.ShapeDtypeStruct((2, 64, D), BF),
            jax.ShapeDtypeStruct((2, 64, D), BF),
            jax.ShapeDtypeStruct((D, F), BF),
            jax.ShapeDtypeStruct((D, F), BF),
            jax.ShapeDtypeStruct((F, D), BF),
        ),
        in_specs=[vmem, vmem, anywhere, anywhere, anywhere, smem, smem, smem],
        out_specs=(vmem, vmem, anywhere, anywhere, anywhere),
        scratch_shapes=[
            pltpu.VMEM((D, F), BF),
            pltpu.VMEM((D, F), BF),
            pltpu.VMEM((F, D), BF),
            pltpu.VMEM((*chunks, D), BF),
            pltpu.VMEM((*chunks, D), BF),
            pltpu.VMEM((D, 2048), BF),
            pltpu.VMEM((D, 2048), BF),
            pltpu.VMEM((D, 2 * F), BF),
            pltpu.VMEM((F, D), BF),
            pltpu.VMEM((*chunks, 2 * F), BF),
            pltpu.VMEM((*chunks, F), BF),
            *scatter_bufs(2 * F), *scatter_bufs(2 * F),
            *scatter_bufs(F), *scatter_bufs(F),
            pltpu.VMEM((*chunks, F), BF),
            pltpu.VMEM((*chunks, 2 * F), BF),
            pltpu.VMEM((2, 64, F), F32),
            pltpu.VMEM((2, 64, F), F32),
            pltpu.VMEM((*chunks, D), BF),
            pltpu.VMEM((*chunks, D), BF),
            pltpu.VMEM((4, 2, 2, 64, D), BF),
            pltpu.VMEM((4, 2, 2, 64, D), BF),
            *[pltpu.VMEM((4, 2, 64, D), BF)] * 4,
            pltpu.SemaphoreType.DMA((NSEM,)),
            pltpu.SemaphoreType.DMA((NSEM,)),
            pltpu.SemaphoreType.DMA((6,)),
        ],
        compiler_params=pltpu.CompilerParams(
            collective_id=0, has_side_effects=True, vmem_limit_bytes=63 * 2**20
        ),
        cost_estimate=pl.CostEstimate(flops=2 * 9 * 2048 * D * F, bytes_accessed=8 * 2**20, transcendentals=0),
    )(
        tokens.reshape(2, 64, D), grad_out.reshape(2, 64, D), gate_weight, up_weight, down_weight,
        gate_mask, up_mask, down_mask.T,
    )
    hbm = pl.BlockSpec(memory_space=pltpu.HBM)
    results = (lo.reshape(BLK, D), ig.reshape(BLK, D), gg, ug, dg)
    return pl.pallas_call(
        hand_over,
        out_shape=tuple(jax.ShapeDtypeStruct(r.shape, r.dtype) for r in results),
        in_specs=[hbm] * 5,
        out_specs=(hbm,) * 5,
        scratch_shapes=[*[pltpu.VMEM(r.shape, r.dtype) for r in results], pltpu.SemaphoreType.DMA((2, 5))],
        compiler_params=pltpu.CompilerParams(vmem_limit_bytes=63 * 2**20),
    )(*results)


def solution(mesh):
    wide, tall = P("row", "col"), P("col", "row")
    return jax.shard_map(
        body,
        mesh=mesh,
        in_specs=(tall, tall, wide, wide, tall, wide, wide, tall),
        out_specs=(tall, tall, wide, wide, tall),
        check_vma=False,
    )
```
